512 devices in a mesh: nodes: 128 (over x, z, core), feat: 4 (over y).
Axes of the slice: x: 4, y: 4, z: 16, core: 2. Of those that a mesh axis runs over, the one named last changes fastest.
Arguments:
- x_batch: bfloat16 [49152, 256], P('nodes', 'feat'), may hold values from -6 to 6
- tiles: bfloat16 [128, 128, 2, 128, 128], P('nodes', None, None, 'feat'), may hold values from -0.0546875 to 0.0546875
- tile_src: int32 [128, 128, 2], P('nodes'), may hold values from 0 to 2
- tile_dst: int32 [128, 128, 2], P(None, 'nodes'), may hold values from 0 to 2
- history: bfloat16 [262144, 256], P('nodes', 'feat'), may hold values from -6 to 6
- halo_ids: int32 [384, 128], P('nodes'), may hold values from 0 to 262143, as said below
- halo_adj: bfloat16 [384, 128, 128], P('nodes'), may hold values from -0.5 to 0.5
- weight: bfloat16 [256, 256], P('feat'), may hold values from -0.375 to 0.375
Outputs:
- new_embed: bfloat16 [49152, 256], P('nodes', 'feat')
The draws below stay inside these ranges and needn't reach their ends.
Inputs may be any that keep to these rules, and one draw needn't show every extreme that they name: `halo_ids`: node i lies on device i // 2048 of nodes. Among the 384 ids of one device's clusters at most 9 lie on any one device, and for every device some one device holds exactly 9 of them.
All inputs are finite; a program needn't handle non-finite values.
Results may differ from the reference program's by a relative error of at most 0.0051.
Values may be sent and summed in bfloat16 or wider, within the bound.
A program may use at most 128 MiB of HBM per device.

```python
import jax
import jax.numpy as jnp
from jax import lax

F = 256
CS = 128
K = 2
CL_DEV = 3
H_CL = 128
NODE_DEV = 2048
PEERS = 128
BATCH_CL = 384
BATCH_NODES = 49152
NODES = 262144


def draw_halo_ids(key, part):
    key = jax.random.fold_in(key, 7)
    halo_total = CL_DEV * H_CL
    slot_cap = 3 * halo_total // PEERS
    spread_count = halo_total - slot_cap

    def one_device(device_key):
        key_hot, key_perm, key_shuffle, key_rows = jax.random.split(device_key, 4)
        hot_owner = jax.random.randint(key_hot, (), 0, PEERS)
        others = jax.random.permutation(key_perm, PEERS - 1)
        positions = jnp.arange(spread_count, dtype=jnp.int32) * (PEERS - 1) // spread_count
        other_owner = (hot_owner + 1 + others[positions]) % PEERS
        owners = jnp.concatenate([jnp.full((slot_cap,), hot_owner, dtype=jnp.int32), other_owner.astype(jnp.int32)])
        owners = jax.random.permutation(key_shuffle, owners)
        local_rows = jax.random.randint(key_rows, (halo_total,), 0, NODE_DEV)
        return owners * NODE_DEV + local_rows
    halo_flat = jax.vmap(one_device)(jax.random.split(key, PEERS))
    return halo_flat.reshape(BATCH_CL, H_CL).astype(jnp.int32)


def with_ends(values, own_key, least, largest):
    longest = values.shape.index(max(values.shape))
    spots = []
    for shift in (0, 1):
        where = [jax.random.randint(jax.random.fold_in(own_key, axis), (), 0, length) for axis, length in enumerate(values.shape)]
        where[longest] = (where[longest] + shift) % values.shape[longest]
        spots.append(tuple(where))
    return values.at[spots[0]].set(least).at[spots[1]].set(largest)


def shard_levels(stream_key, dims, cuts, smallest, high):
    def one(position, blocks):
        steps = jax.random.uniform(jax.random.fold_in(jax.random.fold_in(stream_key, 6), position), (blocks,), jnp.float32, smallest / len(cuts), high / len(cuts))
        return jnp.repeat(jnp.exp(steps), dims[position] // blocks).reshape((-1,) + (1,) * (len(dims) - position - 1))

    loudness = one(*cuts[0])
    for cut in cuts[1:]:
        loudness = loudness * one(*cut)
    return loudness


def normal_values(stream_key, extent, deviation, limit, shards=(), held_as=jnp.bfloat16):
    result = deviation * jax.random.normal(stream_key, extent, jnp.float32)
    if shards:
        result = result * shard_levels(stream_key, extent, shards, -0.22, 0.18)
    return jnp.clip(result, -limit, limit).astype(held_as)


def setup_inputs(seed: int = 0) -> dict:
    key_list = jax.random.split(jax.random.key(seed), 9)
    return {
        "x_batch": normal_values(key_list[0], (BATCH_NODES, F), 1.0, 6.0, ((0, 128), (1, 4))),
        "tiles": normal_values(key_list[1], (PEERS, PEERS, K, CS, CS), (K * PEERS * CS // CL_DEV) ** -0.5, 0.0546875, ((0, 128), (3, 4))),
        "tile_src": with_ends(jax.random.randint(key_list[2], (PEERS, PEERS, K), 0, CL_DEV), jax.random.fold_in(key_list[2], 1), 0, CL_DEV - 1).astype(jnp.int32),
        "tile_dst": with_ends(jax.random.randint(key_list[3], (PEERS, PEERS, K), 0, CL_DEV), jax.random.fold_in(key_list[3], 1), 0, CL_DEV - 1).astype(jnp.int32),
        "history": normal_values(key_list[4], (NODES, F), 1.0, 6.0, ((0, 128), (1, 4))),
        "halo_ids": draw_halo_ids(jax.random.fold_in(key_list[8], 71), 0),
        "halo_adj": normal_values(key_list[6], (BATCH_CL, CS, H_CL), H_CL ** -0.5, 0.5, ((0, 128),)),
        "weight": normal_values(key_list[7], (F, F), F ** -0.5, 0.375, ((0, 4),)),
    }


def reference(x_batch, tiles, tile_src, tile_dst, history, halo_ids, halo_adj, weight):
    cluster_x = x_batch.reshape(BATCH_CL, CS, F).astype(jnp.float32)
    holder_base = jnp.arange(PEERS, dtype=jnp.int32)[:, None] * CL_DEV

    def per_dest(dest):
        blocks = tiles[:, dest].astype(jnp.float32)
        sources = (holder_base + tile_src[:, dest]).astype(jnp.int32)
        source_x = cluster_x[sources]
        products = jnp.einsum('pkij,pkjf->pkif', blocks, source_x, precision=lax.Precision.HIGHEST)
        dst_onehot = (tile_dst[:, dest][..., None] == jnp.arange(CL_DEV, dtype=jnp.int32)).astype(jnp.float32)
        return jnp.einsum('pkc,pkif->cif', dst_onehot, products, precision=lax.Precision.HIGHEST)

    tile_sum = lax.map(per_dest, jnp.arange(PEERS, dtype=jnp.int32)).reshape(BATCH_CL, CS, F)
    halo_x = history[halo_ids].astype(jnp.float32)
    halo_term = jnp.einsum('crh,chf->crf', halo_adj.astype(jnp.float32), halo_x, precision=lax.Precision.HIGHEST)
    aggregate = (tile_sum + halo_term).astype(jnp.bfloat16).reshape(BATCH_NODES, F)
    pre_act = jnp.dot(aggregate, weight, preferred_element_type=jnp.float32)
    return jax.nn.silu(pre_act).astype(jnp.bfloat16)
```

```python
import functools

import jax
import jax.numpy as jnp
from jax import lax
from jax.experimental import pallas as pl
from jax.experimental.pallas import tpu as pltpu
from jax.sharding import PartitionSpec as P

MESH = pl.DeviceIdType.MESH
F32 = jnp.float32
BF16 = jnp.bfloat16
I32 = jnp.int32

X = 4
C = 2
G = X * C
CL = 3
K = 2
CS = 128
SLOTS = 9
PAIR = 16
JP = 5
VR = 48
MARK = 4096


def iota(shape, dim):
    return lax.broadcasted_iota(I32, shape, dim)


def dot_nt(a, b):
    return lax.dot_general(a, b, (((1,), (1,)), ((), ())), preferred_element_type=F32)


def dot_nn(a, b):
    return jnp.dot(a, b, preferred_element_type=F32)


def layer_kernel(
    Z, F, FD, ND,
    x_ref, tiles_ref, src_ref, dst_ref, hist_ref, ids_ref, adj_ref, w_ref, o_ref,
    TV, SV, SSM, XT, XM, WF, ST, ZR, ZR2, AG, ASM, H2, RS, RW, VS, FR, GM, HS, HR,
    LH, OB, PO, PXS, PXR, CHS, CHR, OPS, OPR, OS,
    loc, s_z, r_z, s_g, r_g, s_x, r_x, s_w, r_w, s_t, r_t, s_v, r_v, s_px, r_px, s_c, r_c,
    s_op, r_op, s_rg, r_rg, s_rz, r_rz, s_h, r_h, s_o, r_o,
):
    N = X * Z * C
    FT = F * FD
    RD = CS // F
    RR = CL * RD
    H = Z // 2
    ZB = Z.bit_length() - 1
    NB = ND.bit_length() - 1

    me = lax.axis_index("nodes")
    f = lax.axis_index("feat")
    c = lax.rem(me, C)
    z = lax.rem(me // C, Z)
    x = me // (C * Z)
    oc = 1 - c

    def dev(xx, zz, cc):
        return (xx * Z + zz) * C + cc

    def zp(d):
        return lax.rem(z + d + Z, Z)

    def xp(d):
        return lax.rem(x + d, X)

    def fp(d):
        return lax.rem(f + d, F)

    def rcopy(src, dst, ss, rs, n, ff):
        return pltpu.make_async_remote_copy(
            src_ref=src, dst_ref=dst, send_sem=ss, recv_sem=rs,
            device_id=(n, ff), device_id_type=MESH,
        )

    barrier = pltpu.get_barrier_semaphore()

    def greet(n, ff):
        pl.semaphore_signal(barrier, inc=1, device_id=(n, ff), device_id_type=MESH)

    @pl.loop(1, Z)
    def _(d):
        greet(dev(x, zp(d), c), f)

    for g in range(1, G):
        greet(dev(xp(g // C), z, lax.rem(c + g, C)), f)
    for d in range(1, F):
        greet(me, fp(d))
        greet(dev(x, z, oc), fp(d))

    own_tiles = pltpu.make_async_copy(tiles_ref.at[:, :, c], TV.at[c], loc.at[0])
    own_tiles.start()

    ids = ids_ref[...]
    nid = CL * CS
    row = jnp.concatenate([ids[i : i + 1] for i in range(CL)], axis=1)
    owner = row >> NB
    local = row & (ND - 1)
    o_c = owner & (C - 1)
    o_z = (owner >> 1) & (Z - 1)
    o_x = owner >> (1 + ZB)
    hot = (iota((N, nid), 0) == owner).astype(F32)
    tri = (iota((nid, nid), 0) < iota((nid, nid), 1)).astype(F32).astype(BF16)
    before = dot_nn(hot.astype(BF16), tri)
    rank = jnp.sum(before * hot, axis=0, keepdims=True).astype(I32)
    lane = (o_x * C + o_c) * PAIR + rank
    lane_hot = (iota((G * PAIR, nid), 0) == lane).astype(F32).astype(BF16)
    z_hot = (iota((Z, nid), 0) == o_z).astype(F32)
    hi = (local >> 7).astype(F32)
    lo = (local & 127).astype(F32)
    table = 128.0 * dot_nt((z_hot * hi).astype(BF16), lane_hot) + dot_nt(
        (z_hot * lo).astype(BF16), lane_hot
    )
    asked = dot_nt(z_hot.astype(BF16), lane_hot)
    holder = iota((1, N), 1)
    h_z = (holder >> 1) & (Z - 1)
    h_l = ((holder >> (1 + ZB)) * C + (holder & 1)) * PAIR + SLOTS
    z_hold = (iota((Z, N), 0) == h_z).astype(F32)
    for k in range(K):
        l_hold = (iota((G * PAIR, N), 0) == h_l + k).astype(F32).astype(BF16)
        code = dst_ref[k : k + 1, :].astype(F32)
        table += dot_nt((z_hold * code).astype(BF16), l_hold)
    table = table.astype(I32) + jnp.where(asked > 0.5, 0, MARK)
    for i in range(Z):
        ST[i] = table[i : i + 1]

    pl.semaphore_wait(barrier, Z - 1 + G - 1 + 2 * (F - 1))

    def z_send(d):
        return rcopy(ST.at[zp(d)], ZR.at[z], s_z.at[d], r_z.at[z], dev(x, zp(d), c), f)

    def z_recv(d):
        return rcopy(ST.at[z], ZR.at[zp(d)], s_z.at[d], r_z.at[zp(d)], dev(x, zp(d), c), f)

    @pl.loop(1, Z)
    def _(d):
        z_send(d).start()

    sib = dev(x, z, oc)
    t_send = rcopy(tiles_ref.at[:, :, oc], TV.at[c], s_t.at[0], r_t.at[0], sib, f)
    v_send = rcopy(src_ref, SV.at[c], s_v.at[0], r_v.at[0], sib, f)
    v_send.start()
    t_send.start()

    def x_peer(e):
        return dev(x, z, lax.rem(c + e, C)), lax.rem(c + e, C)

    def x_send(d, e):
        n, _ = x_peer(e)
        return rcopy(
            x_ref, XT.at[c, pl.ds(pl.multiple_of(f * FD, FD), FD)],
            s_x.at[d, e], r_x.at[c, f], n, fp(d),
        )

    def x_recv(d, e):
        n, cc = x_peer(e)
        ff = fp(d)
        return rcopy(
            x_ref, XT.at[cc, pl.ds(pl.multiple_of(ff * FD, FD), FD)],
            s_x.at[d, e], r_x.at[cc, ff], n, ff,
        )

    x_pairs = [(d, e) for e in range(C) for d in range(F) if (d, e) != (0, 0)]
    for d, e in x_pairs:
        x_send(d, e).start()

    def w_send(d):
        return rcopy(w_ref, WF.at[f], s_w.at[d], r_w.at[f], me, fp(d))

    def w_recv(d):
        return rcopy(w_ref, WF.at[fp(d)], s_w.at[d], r_w.at[fp(d)], me, fp(d))

    for d in range(1, F):
        w_send(d).start()

    XT[c, pl.ds(pl.multiple_of(f * FD, FD), FD)] = x_ref[...]
    WF[f] = w_ref[...]
    SV[c] = src_ref[...]
    ZR[z] = ST[z]

    @pl.loop(1, Z)
    def _(d):
        z_recv(d).wait_recv()

    for i in range(Z):
        ZR2[i : i + 1, :] = ZR[i]

    def g_peer(g):
        return xp(g // C), lax.rem(c + g, C)

    def g_send(g):
        gx, gc = g_peer(g)
        return rcopy(ZR2, AG.at[c, x], s_g.at[g], r_g.at[c, x], dev(gx, z, gc), f)

    def g_recv(g):
        gx, gc = g_peer(g)
        return rcopy(ZR2, AG.at[gc, gx], s_g.at[g], r_g.at[gc, gx], dev(gx, z, gc), f)

    for g in range(1, G):
        g_send(g).start()
    AG[c, x] = ZR2[...]

    for d, e in x_pairs:
        x_recv(d, e).wait_recv()
    rcopy(src_ref, SV.at[oc], s_v.at[0], r_v.at[0], sib, f).wait_recv()
    src_copy = pltpu.make_async_copy(SV, SSM, loc.at[1])
    src_copy.start()
    for h in range(C):
        for s in range(CL):
            XM[h, s * CS : (s + 1) * CS, :] = XT[h, :, s * CS : (s + 1) * CS].T
    zero = jnp.zeros((FD, ND), BF16)
    hist = hist_ref[...]
    H2[0, 0:FD] = hist
    H2[0, FD : 2 * FD] = zero
    H2[1, 0:FD] = zero
    H2[1, FD : 2 * FD] = hist

    for g in range(1, G):
        g_recv(g).wait_recv()
    code_copy = pltpu.make_async_copy(AG.at[c], ASM, loc.at[2])
    code_copy.start()
    rcopy(tiles_ref.at[:, :, oc], TV.at[oc], s_t.at[0], r_t.at[0], sib, f).wait_recv()
    own_tiles.wait()
    src_copy.wait()
    code_copy.wait()

    def dirs_of(r):
        return (0,) if r in (0, H) else (0, 1)

    def at(r, d):
        return zp(r) if d == 0 else zp(-r)

    KR = K * RD

    def products(r):
        dirs = dirs_of(r)
        count = len(dirs) * X

        def place(b):
            bx = lax.rem(b, X)
            step = jnp.where(b < X, r, Z - r)
            return lax.rem(x + bx, X), lax.rem(z + step, Z)

        def gather(b, carry):
            tx, tz = place(b)
            n = dev(tx, tz, c)
            for h in range(C):
                for k in range(K):
                    tile = TV[h, tx, tz, k]
                    src = SSM[h, k, n]
                    rows = pl.ds(pl.multiple_of(b * KR + k * RD, RD), RD)
                    for s in range(CL):
                        LH[h, rows, s * CS : (s + 1) * CS] = jnp.where(
                            src == s, tile, jnp.zeros_like(tile)
                        )
            return carry

        lax.fori_loop(0, count, gather, 0)
        m = count * KR
        for h in range(C):
            OB[h, 0:m] = dot_nn(LH[h, 0:m], XM[h])

        def combine(b, carry):
            tx, tz = place(b)
            bx = lax.rem(b, X)
            bd = b // X
            for d in range(CL):
                total = jnp.zeros((RD, FT), F32)
                for h in range(C):
                    for k in range(K):
                        part = OB[h, pl.ds(pl.multiple_of(b * KR + k * RD, RD), RD)]
                        code = ASM[tx, tz, x * (C * PAIR) + h * PAIR + SLOTS + k] - MARK
                        total += jnp.where(code == d, part, jnp.zeros_like(part))
                PO[r, bd, bx, d * RD : (d + 1) * RD] = total
            return carry

        lax.fori_loop(0, count, combine, 0)

    def px(r, d, side):
        to = xp(1 if side == 0 else X - 1)
        return rcopy(
            PXS.at[r, d, side], PXR.at[r, d, side], s_px.at[r, d, side], r_px.at[r, d, side],
            dev(to, z, c), f,
        )

    def send_x(r):
        for d in dirs_of(r):
            for side, bx in ((0, 1), (1, X - 1)):
                PXS[r, d, side] = PO[r, d, bx].astype(BF16)
                px(r, d, side).start()

    def chain(ph, d, r):
        to = zp(1 if d == 0 else -1)
        return rcopy(
            CHS.at[ph, d, r - 1], CHR.at[ph, d, r - 1], s_c.at[ph, d, r - 1],
            r_c.at[ph, d, r - 1], dev(x, to, c), f,
        )

    def live(ph, d, r):
        return r < H or (r == H and d == ph)

    def own(ph, r, d):
        pd = 0 if r in (0, H) else d
        if ph == 0:
            return PO[r, pd, 2]
        return (
            PO[r, pd, 0] + PXR[r, pd, 0].astype(F32) + PXR[r, pd, 1].astype(F32)
        )

    def chain_step(ph, r):
        if ph == 1:
            for d in dirs_of(r):
                for side in range(2):
                    px(r, d, side).wait_recv()
        for d in range(2):
            if not live(ph, d, r):
                continue
            total = own(ph, r, d)
            if live(ph, d, r + 1):
                chain(ph, d, r + 1).wait_recv()
                total = total + CHR[ph, d, r].astype(F32)
            CHS[ph, d, r - 1] = total.astype(BF16)
            chain(ph, d, r).start()

    def chain_end(ph):
        total = own(ph, 0, 0)
        for d in range(2):
            chain(ph, d, 1).wait_recv()
            total = total + CHR[ph, d, 0].astype(F32)
        return total

    def rg_send(g):
        gx, gc = g_peer(g)
        return rcopy(RS.at[gc, gx], RW.at[c, x], s_rg.at[g], r_rg.at[c, x], dev(gx, z, gc), f)

    def rg_recv(g):
        gx, gc = g_peer(g)
        return rcopy(RS.at[c, x], RW.at[gc, gx], s_rg.at[g], r_rg.at[gc, gx], dev(gx, z, gc), f)

    def halo_serve():
        asks = AG[...].reshape(G * Z, G * PAIR).astype(F32)
        lanes = iota((G * Z, G * PAIR), 1)
        base = x * (C * PAIR) + c * PAIR
        KB = min(512, ND)
        for j in range(JP):
            total = jnp.zeros((G * Z, 2 * FD), F32)
            for par in range(2):
                s = 2 * j + par
                if s >= SLOTS:
                    continue
                want = jnp.sum(
                    jnp.where(lanes == base + s, asks, 0.0), axis=1, keepdims=True
                ).astype(I32)
                for b in range(ND // KB):
                    pick = (iota((G * Z, KB), 1) + b * KB == want).astype(F32).astype(BF16)
                    total += dot_nt(pick, H2[par, :, b * KB : (b + 1) * KB])
            RS[:, :, j] = total.astype(BF16).reshape(C, X, Z, 2 * FD)
        for g in range(1, G):
            rg_send(g).start()
        RW[c, x] = RS[c, x]

    def rz_send(d):
        return rcopy(VS.at[zp(d)], FR.at[z], s_rz.at[d], r_rz.at[z], dev(x, zp(d), c), f)

    def rz_recv(d):
        return rcopy(VS.at[z], FR.at[zp(d)], s_rz.at[d], r_rz.at[zp(d)], dev(x, zp(d), c), f)

    def halo_relay():
        for g in range(1, G):
            rg_recv(g).wait_recv()
        rows = RW[...].reshape(G * JP * Z, 2 * FD)
        shape = (VR, G * JP * Z)
        for i in range(Z):
            pick = (iota(shape, 1) == iota(shape, 0) * Z + i).astype(F32).astype(BF16)
            VS[i] = dot_nn(pick, rows).astype(BF16)

        @pl.loop(1, Z)
        def _(d):
            rz_send(d).start()

        FR[z] = VS[z]

    def halo_matrices():
        spot = o_z * VR + (o_c * X + o_x) * JP + (rank >> 1)
        for cl in range(CL):
            cols = slice(cl * CS, (cl + 1) * CS)
            hit = iota((Z * VR, CS), 0) == spot[:, cols]
            odd = rank[:, cols] & 1
            for par in range(2):
                pick = jnp.where(hit, (odd == par).astype(F32), 0.0).astype(BF16)
                GM[par, cols] = dot_nt(adj_ref[cl], pick).astype(BF16)

    def h_send(d):
        return rcopy(HS.at[fp(d)], HR.at[f], s_h.at[d], r_h.at[f], me, fp(d))

    def h_recv(d):
        return rcopy(HS.at[f], HR.at[fp(d)], s_h.at[d], r_h.at[fp(d)], me, fp(d))

    def halo_finish():
        @pl.loop(1, Z)
        def _(d):
            rz_recv(d).wait_recv()

        rows = FR[...].reshape(Z * VR, 2 * FD)
        even = dot_nn(GM[0], rows)
        odd = dot_nn(GM[1], rows)
        halo = even[:, 0:FD] + odd[:, FD : 2 * FD]
        for i in range(F):
            for cl in range(CL):
                at_row = cl * CS + i * RD
                HS[i, cl * RD : (cl + 1) * RD] = halo[at_row : at_row + RD]
        for d in range(1, F):
            h_send(d).start()
        HR[f] = HS[f]

    products(H)
    send_x(H)
    chain_step(0, H)
    products(H - 1)
    send_x(H - 1)
    halo_serve()
    halo_matrices()
    for r in range(H - 1, 0, -1):
        chain_step(0, r)
        chain_step(1, r + 1)
        products(r - 1)
        send_x(r - 1)
        if r == H - 1:
            halo_relay()
    OPS[...] = chain_end(0)
    op = rcopy(OPS, OPR, s_op.at[0], r_op.at[0], dev(xp(2), z, c), f)
    op.start()
    chain_step(1, 1)
    halo_finish()

    for d in range(1, F):
        w_recv(d).wait_recv()
    for d in range(1, F):
        h_recv(d).wait_recv()

    def split(v):
        top = v.astype(BF16)
        return top, (v - top.astype(F32)).astype(BF16)

    act = jnp.zeros((RR, FT), F32)
    for i in range(F):
        top, rest = split(HR[i])
        act += dot_nn(top, WF[i]) + dot_nn(rest, WF[i])
    for side in range(2):
        px(0, 0, side).wait_recv()
    total = chain_end(1)
    op.wait_recv()
    top, rest = split(total + OPR[...])
    weight = WF[...].reshape(FT, FT)
    act += dot_nn(top, weight) + dot_nn(rest, weight)
    out = act / (1.0 + jnp.exp(-act))

    def o_send(d):
        return rcopy(OS.at[fp(d)], o_ref.at[f], s_o.at[d], r_o.at[f], me, fp(d))

    def o_recv(d):
        return rcopy(OS.at[f], o_ref.at[fp(d)], s_o.at[d], r_o.at[fp(d)], me, fp(d))

    for i in range(F):
        OS[i] = out[:, i * FD : (i + 1) * FD].astype(BF16)
    for d in range(1, F):
        o_send(d).start()
    o_ref[f] = OS[f]

    @pl.loop(1, Z)
    def _(d):
        z_send(d).wait_send()
        rz_send(d).wait_send()

    for g in range(1, G):
        g_send(g).wait_send()
        rg_send(g).wait_send()
    t_send.wait_send()
    v_send.wait_send()
    for d, e in x_pairs:
        x_send(d, e).wait_send()
    for d in range(1, F):
        w_send(d).wait_send()
        h_send(d).wait_send()
        o_send(d).wait_send()
    for r in range(H + 1):
        for d in dirs_of(r):
            for side in range(2):
                px(r, d, side).wait_send()
        for ph in range(2):
            for d in range(2):
                if r > 0 and live(ph, d, r):
                    chain(ph, d, r).wait_send()
    op.wait_send()
    for d in range(1, F):
        o_recv(d).wait_recv()


def per_device(F, x_batch, tiles, tile_src, tile_dst, history, halo_ids, halo_adj, weight):
    N = tile_dst.shape[0]
    Z = N // G
    FD = x_batch.shape[1]
    FT = F * FD
    ND = history.shape[0]
    RD = CS // F
    RR = CL * RD
    H = Z // 2
    src_t = tile_src.reshape(N, K).T
    dst_t = tile_dst.reshape(N, K).T
    tiles_v = tiles.reshape(X, Z, C, K, RD, CS)
    vmem = pl.BlockSpec(memory_space=pltpu.VMEM)
    dma = pltpu.SemaphoreType.DMA
    mmax = 2 * X * K * RD
    out = pl.pallas_call(
        functools.partial(layer_kernel, Z, F, FD, ND),
        out_shape=jax.ShapeDtypeStruct((F, RR, FD), BF16),
        in_specs=[vmem, pl.BlockSpec(memory_space=pl.ANY)] + [vmem] * 6,
        out_specs=vmem,
        scratch_shapes=[
            pltpu.VMEM((C, X, Z, K, RD, CS), BF16),
            pltpu.VMEM((C, K, N), I32),
            pltpu.SMEM((C, K, N), I32),
            pltpu.VMEM((C, FT, CL * CS), BF16),
            pltpu.VMEM((C, CL * CS, FT), BF16),
            pltpu.VMEM((F, FD, FT), BF16),
            pltpu.VMEM((Z, 1, G * PAIR), I32),
            pltpu.VMEM((Z, 1, G * PAIR), I32),
            pltpu.VMEM((Z, G * PAIR), I32),
            pltpu.VMEM((C, X, Z, G * PAIR), I32),
            pltpu.SMEM((X, Z, G * PAIR), I32),
            pltpu.VMEM((2, 2 * FD, ND), BF16),
            pltpu.VMEM((C, X, JP, Z, 2 * FD), BF16),
            pltpu.VMEM((C, X, JP, Z, 2 * FD), BF16),
            pltpu.VMEM((Z, VR, 2 * FD), BF16),
            pltpu.VMEM((Z, VR, 2 * FD), BF16),
            pltpu.VMEM((2, CL * CS, Z * VR), BF16),
            pltpu.VMEM((F, RR, FD), F32),
            pltpu.VMEM((F, RR, FD), F32),
            pltpu.VMEM((C, mmax, CL * CS), BF16),
            pltpu.VMEM((C, mmax, FT), F32),
            pltpu.VMEM((H + 1, 2, X, RR, FT), F32),
            pltpu.VMEM((H + 1, 2, 2, RR, FT), BF16),
            pltpu.VMEM((H + 1, 2, 2, RR, FT), BF16),
            pltpu.VMEM((2, 2, H, RR, FT), BF16),
            pltpu.VMEM((2, 2, H, RR, FT), BF16),
            pltpu.VMEM((RR, FT), F32),
            pltpu.VMEM((RR, FT), F32),
            pltpu.VMEM((F, RR, FD), BF16),
            dma((3,)),
            dma((Z,)), dma((Z,)),
            dma((G,)), dma((C, X)),
            dma((F, C)), dma((C, F)),
            dma((F,)), dma((F,)),
            dma((1,)), dma((1,)),
            dma((1,)), dma((1,)),
            dma((H + 1, 2, 2)), dma((H + 1, 2, 2)),
            dma((2, 2, H)), dma((2, 2, H)),
            dma((1,)), dma((1,)),
            dma((G,)), dma((C, X)),
            dma((Z,)), dma((Z,)),
            dma((F,)), dma((F,)),
            dma((F,)), dma((F,)),
        ],
        compiler_params=pltpu.CompilerParams(
            collective_id=0, has_side_effects=True, vmem_limit_bytes=48 * 1024 * 1024
        ),
        name="layer",
    )(x_batch.T, tiles_v, src_t, dst_t, history.T, halo_ids, halo_adj, weight)
    return out.reshape(F, CL, RD, FD).transpose(1, 0, 2, 3).reshape(CL * CS, FD)


def solution(mesh):
    return jax.shard_map(
        functools.partial(per_device, mesh.shape["feat"]),
        mesh=mesh,
        in_specs=(
            P("nodes", "feat"),
            P("nodes", None, None, "feat", None),
            P("nodes", None, None),
            P(None, "nodes", None),
            P("nodes", "feat"),
            P("nodes", None),
            P("nodes", None, None),
            P("feat", None),
        ),
        out_specs=P("nodes", "feat"),
        check_vma=False,
    )
```

```python
import functools

import jax
import jax.numpy as jnp
from jax import lax
from jax.experimental import pallas as pl
from jax.experimental.pallas import tpu as pltpu
from jax.sharding import PartitionSpec as P

MESH = pl.DeviceIdType.MESH
F32 = jnp.float32
BF16 = jnp.bfloat16
I32 = jnp.int32

X = 4
C = 2
G = X * C
CL = 3
K = 2
CS = 128
CUT = 0
STEP0 = (1, 1, 1, 1, 1, 1, 1, 1)
STEP1 = (1, 1, 1, 1, 1, 1, 1, 1)
ORDER = [
    "P8", "X8", "A8", "W0", "H0", "H1", "H2", "H3", "H4", "H5", "H6", "H7", "G0",
    "P7", "X7", "A7", "B8", "P6", "X6", "A6", "B7", "R0", "S0",
    "P5", "X5", "A5", "B6", "S1", "P4", "X4", "A4", "B5", "S2", "S3",
    "P3", "X3", "A3", "B4", "S4", "P2", "X2", "A2", "B3", "P1", "X1", "A1", "B2",
    "P0", "X0", "E0", "F0", "B1",
]
SLOTS = 9
PAIR = 16
JP = 5
VR = 48
MARK = 4096


def iota(shape, dim):
    return lax.broadcasted_iota(I32, shape, dim)


def dot_nt(a, b):
    return lax.dot_general(a, b, (((1,), (1,)), ((), ())), preferred_element_type=F32)


def dot_nn(a, b):
    return jnp.dot(a, b, preferred_element_type=F32)


def layer_kernel(
    Z, F, FD, ND, CUT,
    x_hbm, tiles_ref, src_hbm, dst_hbm, hist_hbm, ids_hbm, adj_hbm, w_hbm, o_ref,
    XI, SI, DI, HI, II, AI, WI,
    TV, SV, SSM, XT, XM, WF, ST, ZR, ZR2, AG, ASM, H2, WB, HACC, PK, RS, RW, VS, FR, GM, HS, HR,
    LH, OB, PO, PXS, PXR, CHS, CHR, OPS, OPR, OS,
    loc, s_z, r_z, s_g, r_g, s_x, r_x, s_w, r_w, s_t, r_t, s_v, r_v, s_px, r_px, s_c, r_c,
    s_op, r_op, s_rg, r_rg, s_rz, r_rz, s_h, r_h, s_o, r_o,
):
    N = X * Z * C
    FT = F * FD
    RD = CS // F
    RR = CL * RD
    H = Z // 2
    ZB = Z.bit_length() - 1
    NB = ND.bit_length() - 1

    me = lax.axis_index("nodes")
    f = lax.axis_index("feat")
    c = lax.rem(me, C)
    z = lax.rem(me // C, Z)
    x = me // (C * Z)
    oc = 1 - c
    sib = (x * Z + z) * C + oc

    def dev(xx, zz, cc):
        return (xx * Z + zz) * C + cc

    def zp(d):
        return lax.rem(z + d + Z, Z)

    def xp(d):
        return lax.rem(x + d, X)

    def fp(d):
        return lax.rem(f + d, F)

    def rcopy(src, dst, ss, rs, n, ff):
        return pltpu.make_async_remote_copy(
            src_ref=src, dst_ref=dst, send_sem=ss, recv_sem=rs,
            device_id=(n, ff), device_id_type=MESH,
        )

    begun = {}

    class Exchange:
        def __init__(self, steps, send, recv=None, rolled=False):
            self.steps, self.send, self.recv = steps, send, recv or send
            self.rolled = rolled
            self.received = False

        def each(self, act):
            if self.rolled:
                pl.loop(self.steps[0], self.steps[-1] + 1)(act)
            else:
                for step in self.steps:
                    act(step)

        def begin(self):
            begun[id(self)] = self
            self.each(lambda step: self.send(step).start())

        def arrive(self):
            self.received = True
            self.each(lambda step: self.recv(step).wait_recv())

        def finish(self):
            self.each(lambda step: self.send(step).wait_send())

    def finish_all():
        for e in begun.values():
            if not e.received:
                e.arrive()
            e.finish()

    loads = [
        pltpu.make_async_copy(src, dst, loc.at[i])
        for i, (src, dst) in enumerate(
            [
                (ids_hbm, II), (dst_hbm, DI), (src_hbm, SI), (x_hbm, XI), (w_hbm, WI),
                (hist_hbm, HI), (adj_hbm, AI), (tiles_ref.at[:, :, c], TV.at[c]),
            ]
        )
    ]
    for load in loads:
        load.start()
    l_ids, l_dst, l_src, l_x, l_w, l_hist, l_adj, own_tiles = loads

    barrier = pltpu.get_barrier_semaphore()

    def greet(n, ff):
        pl.semaphore_signal(barrier, inc=1, device_id=(n, ff), device_id_type=MESH)

    @pl.loop(1, Z)
    def _(d):
        greet(dev(x, zp(d), c), f)

    for g in range(1, G):
        greet(dev(xp(g // C), z, lax.rem(c + g, C)), f)
    for d in range(1, F):
        greet(me, fp(d))
        greet(sib, fp(d))

    l_ids.wait()
    l_dst.wait()
    ids = II[...]
    nid = CL * CS
    row = jnp.concatenate([ids[i : i + 1] for i in range(CL)], axis=1)
    owner = row >> NB
    local = row & (ND - 1)
    o_c = owner & (C - 1)
    o_z = (owner >> 1) & (Z - 1)
    o_x = owner >> (1 + ZB)
    hot = (iota((N, nid), 0) == owner).astype(F32)
    tri = (iota((nid, nid), 0) < iota((nid, nid), 1)).astype(F32).astype(BF16)
    before = dot_nn(hot.astype(BF16), tri)
    rank = jnp.sum(before * hot, axis=0, keepdims=True).astype(I32)
    lane = (o_x * C + o_c) * PAIR + rank
    lane_hot = (iota((G * PAIR, nid), 0) == lane).astype(F32).astype(BF16)
    z_hot = (iota((Z, nid), 0) == o_z).astype(F32)
    hi = (local >> 7).astype(F32)
    lo = (local & 127).astype(F32)
    table = 128.0 * dot_nt((z_hot * hi).astype(BF16), lane_hot) + dot_nt(
        (z_hot * lo).astype(BF16), lane_hot
    )
    asked = dot_nt(z_hot.astype(BF16), lane_hot)
    holder = iota((1, N), 1)
    h_z = (holder >> 1) & (Z - 1)
    h_l = ((holder >> (1 + ZB)) * C + (holder & 1)) * PAIR + SLOTS
    z_hold = (iota((Z, N), 0) == h_z).astype(F32)
    for k in range(K):
        l_hold = (iota((G * PAIR, N), 0) == h_l + k).astype(F32).astype(BF16)
        code = DI[k : k + 1, :].astype(F32)
        table += dot_nt((z_hold * code).astype(BF16), l_hold)
    table = table.astype(I32) + jnp.where(asked > 0.5, 0, MARK)
    for i in range(Z):
        ST[i] = table[i : i + 1]

    if CUT == 1:
        for load in loads[2:]:
            load.wait()
    pl.semaphore_wait(barrier, Z - 1 + G - 1 + 2 * (F - 1))
    if CUT == 1:
        o_ref[...] = jnp.zeros_like(o_ref)
        return

    hop_z = Exchange(
        range(1, Z),
        lambda d: rcopy(ST.at[zp(d)], ZR.at[z], s_z.at[d], r_z.at[z], dev(x, zp(d), c), f),
        lambda d: rcopy(ST.at[z], ZR.at[zp(d)], s_z.at[d], r_z.at[zp(d)], dev(x, zp(d), c), f),
        rolled=True,
    )
    hop_z.begin()

    t_swap = Exchange(
        [0],
        lambda _: rcopy(tiles_ref.at[:, :, oc], TV.at[c], s_t.at[0], r_t.at[0], sib, f),
        lambda _: rcopy(tiles_ref.at[:, :, oc], TV.at[oc], s_t.at[0], r_t.at[0], sib, f),
    )
    v_swap = Exchange(
        [0],
        lambda _: rcopy(src_hbm, SV.at[c], s_v.at[0], r_v.at[0], sib, f),
        lambda _: rcopy(src_hbm, SV.at[oc], s_v.at[0], r_v.at[0], sib, f),
    )

    def x_rows(cc, ff):
        return XT.at[cc, pl.ds(pl.multiple_of(ff * FD, FD), FD)]

    def x_core(e):
        return lax.rem(c + e, C)

    x_swap = Exchange(
        [(d, e) for e in range(C) for d in range(F) if (d, e) != (0, 0)],
        lambda p: rcopy(
            x_hbm, x_rows(c, f), s_x.at[p], r_x.at[c, f], dev(x, z, x_core(p[1])), fp(p[0])
        ),
        lambda p: rcopy(
            x_hbm, x_rows(x_core(p[1]), fp(p[0])), s_x.at[p], r_x.at[x_core(p[1]), fp(p[0])],
            dev(x, z, x_core(p[1])), fp(p[0]),
        ),
    )
    w_swap = Exchange(
        range(1, F),
        lambda d: rcopy(w_hbm, WF.at[f], s_w.at[d], r_w.at[f], me, fp(d)),
        lambda d: rcopy(w_hbm, WF.at[fp(d)], s_w.at[d], r_w.at[fp(d)], me, fp(d)),
    )
    v_swap.begin()
    x_swap.begin()
    t_swap.begin()
    w_swap.begin()
    l_src.wait()
    l_x.wait()
    l_w.wait()
    XT[c, pl.ds(pl.multiple_of(f * FD, FD), FD)] = XI[...]
    WF[f] = WI[...]
    SV[c] = SI[...]
    ZR[z] = ST[z]

    l_hist.wait()
    hist = HI[...]
    zero = jnp.zeros((FD, ND), BF16)
    H2[0] = jnp.concatenate([hist, zero], axis=0).T
    H2[1] = jnp.concatenate([zero, hist], axis=0).T
    l_adj.wait()
    spot = o_z * VR + (o_c * X + o_x) * JP + (rank >> 1)
    for cl in range(CL):
        cols = slice(cl * CS, (cl + 1) * CS)
        hit = iota((Z * VR, CS), 0) == spot[:, cols]
        odd = rank[:, cols] & 1
        for par in range(2):
            pick = jnp.where(hit, (odd == par).astype(F32), 0.0).astype(BF16)
            GM[par, cols] = dot_nt(AI[cl], pick).astype(BF16)

    def relay_rows(i, carry):
        shape = (VR, G * JP * Z)
        pick = (iota(shape, 1) == iota(shape, 0) * Z + i).astype(F32).astype(BF16)
        PK[pl.ds(pl.multiple_of(i * VR, VR), VR)] = pick
        return carry

    lax.fori_loop(0, Z, relay_rows, 0)

    hop_z.arrive()
    for i in range(Z):
        ZR2[i : i + 1, :] = ZR[i]

    def g_peer(g):
        return xp(g // C), lax.rem(c + g, C)

    def g_send(g):
        gx, gc = g_peer(g)
        return rcopy(ZR2, AG.at[c, x], s_g.at[g], r_g.at[c, x], dev(gx, z, gc), f)

    def g_recv(g):
        gx, gc = g_peer(g)
        return rcopy(ZR2, AG.at[gc, gx], s_g.at[g], r_g.at[gc, gx], dev(gx, z, gc), f)

    hop_g = Exchange(range(1, G), g_send, g_recv)
    hop_g.begin()
    AG[c, x] = ZR2[...]
    if CUT == 2:
        hop_g.arrive()
        own_tiles.wait()
        finish_all()
        o_ref[...] = jnp.zeros_like(o_ref)
        return

    x_swap.arrive()
    v_swap.arrive()
    src_copy = pltpu.make_async_copy(SV, SSM, loc.at[8])
    src_copy.start()
    for h in range(C):
        for s in range(CL):
            XM[h, s * CS : (s + 1) * CS, :] = XT[h, :, s * CS : (s + 1) * CS].T
    hop_g.arrive()
    code_copy = pltpu.make_async_copy(AG.at[c], ASM, loc.at[9])
    code_copy.start()
    t_swap.arrive()
    own_tiles.wait()
    src_copy.wait()
    code_copy.wait()
    if CUT == 3:
        finish_all()
        o_ref[...] = jnp.zeros_like(o_ref)
        return

    def dirs_of(r):
        return (0,) if r in (0, H) else (0, 1)

    KR = K * RD

    def products(r):
        count = len(dirs_of(r)) * X

        def place(b):
            bx = lax.rem(b, X)
            step = jnp.where(b < X, r, Z - r)
            return lax.rem(x + bx, X), lax.rem(z + step, Z)

        def gather(b, carry):
            tx, tz = place(b)
            n = dev(tx, tz, c)
            for h in range(C):
                for k in range(K):
                    tile = TV[h, tx, tz, k]
                    src = SSM[h, k, n]
                    rows = pl.ds(pl.multiple_of(b * KR + k * RD, RD), RD)
                    for s in range(CL):
                        LH[h, rows, s * CS : (s + 1) * CS] = jnp.where(
                            src == s, tile, jnp.zeros_like(tile)
                        )
            return carry

        lax.fori_loop(0, count, gather, 0)
        m = count * KR
        for h in range(C):
            OB[h, 0:m] = dot_nn(LH[h, 0:m], XM[h])

        def combine(b, carry):
            tx, tz = place(b)
            bx = lax.rem(b, X)
            bd = b // X
            for d in range(CL):
                total = jnp.zeros((RD, FT), F32)
                for h in range(C):
                    for k in range(K):
                        part = OB[h, pl.ds(pl.multiple_of(b * KR + k * RD, RD), RD)]
                        code = ASM[tx, tz, x * (C * PAIR) + h * PAIR + SLOTS + k] - MARK
                        total += jnp.where(code == d, part, jnp.zeros_like(part))
                PO[r, bd, bx, d * RD : (d + 1) * RD] = total
            return carry

        lax.fori_loop(0, count, combine, 0)

    def px_copy(p):
        to = xp(1 if p[2] == 0 else X - 1)
        return rcopy(PXS.at[p], PXR.at[p], s_px.at[p], r_px.at[p], dev(to, z, c), f)

    px = {
        (r, d, side): Exchange([(r, d, side)], px_copy)
        for r in range(H + 1) for d in dirs_of(r) for side in range(2)
    }

    def send_x(r):
        for d in dirs_of(r):
            for side, bx in ((0, 1), (1, X - 1)):
                PXS[r, d, side] = PO[r, d, bx].astype(BF16)
                px[r, d, side].begin()

    def live(ph, d, r):
        return r < H or (r == H and d == ph)

    def step_of(ph, r):
        return (STEP0, STEP1)[ph][r - 1]

    def inputs(ph, d, r):
        return [q for q in range(H, r, -1) if live(ph, d, q) and q - step_of(ph, q) == r]

    def chain_copy(p):
        ph, d, at_r = p
        step = step_of(ph, at_r + 1)
        to = zp(step if d == 0 else -step)
        return rcopy(CHS.at[p], CHR.at[p], s_c.at[p], r_c.at[p], dev(x, to, c), f)

    chain = {
        (ph, d, r): Exchange([(ph, d, r - 1)], chain_copy)
        for ph in range(2) for d in range(2) for r in range(1, H + 1) if live(ph, d, r)
    }

    def own(ph, r, d):
        pd = 0 if r in (0, H) else d
        if ph == 0:
            return PO[r, pd, 2]
        return (
            PO[r, pd, 0] + PXR[r, pd, 0].astype(F32) + PXR[r, pd, 1].astype(F32)
        )

    def chain_step(ph, r):
        if ph == 1:
            for d in dirs_of(r):
                for side in range(2):
                    px[r, d, side].arrive()
        for d in range(2):
            if not live(ph, d, r):
                continue
            total = own(ph, r, d)
            for q in inputs(ph, d, r):
                chain[ph, d, q].arrive()
                total = total + CHR[ph, d, q - 1].astype(F32)
            CHS[ph, d, r - 1] = total.astype(BF16)
            chain[ph, d, r].begin()

    def chain_end(ph):
        total = own(ph, 0, 0)
        for d in range(2):
            for q in inputs(ph, d, 0):
                chain[ph, d, q].arrive()
                total = total + CHR[ph, d, q - 1].astype(F32)
        return total

    def rg_send(g):
        gx, gc = g_peer(g)
        return rcopy(RS.at[gc, gx], RW.at[c, x], s_rg.at[g], r_rg.at[c, x], dev(gx, z, gc), f)

    def rg_recv(g):
        gx, gc = g_peer(g)
        return rcopy(RS.at[c, x], RW.at[gc, gx], s_rg.at[g], r_rg.at[gc, gx], dev(gx, z, gc), f)

    back_g = Exchange(range(1, G), rg_send, rg_recv)

    def halo_wants():
        asks = AG[...].reshape(G * Z, G * PAIR).astype(F32)
        lanes = iota((G * Z, G * PAIR), 1)
        base = x * (C * PAIR) + c * PAIR
        for s in range(SLOTS):
            want = jnp.sum(jnp.where(lanes == base + s, asks, 0.0), axis=1, keepdims=True)
            WB[s] = jnp.broadcast_to(want, (G * Z, CS)).astype(I32)

    KB = min(512, ND)

    def halo_part(par, b):
        slots = range(par, SLOTS, 2)
        wide = iota((G * Z, KB), 1) + b * KB
        pick = jnp.concatenate(
            [
                (wide == jnp.concatenate([WB[s]] * (KB // CS), axis=1)).astype(F32).astype(BF16)
                for s in slots
            ],
            axis=0,
        )
        rows = len(slots) * G * Z
        got = dot_nn(pick, H2[par, b * KB : (b + 1) * KB])
        HACC[0:rows] = got if b == 0 and par == 0 else HACC[0:rows] + got

    def halo_answer():
        for j in range(JP):
            got = HACC[j * G * Z : (j + 1) * G * Z].astype(BF16)
            RS[:, :, j] = got.reshape(C, X, Z, 2 * FD)
        back_g.begin()
        RW[c, x] = RS[c, x]

    back_z = [
        Exchange(
            ds,
            lambda d: rcopy(VS.at[zp(d)], FR.at[z], s_rz.at[d], r_rz.at[z], dev(x, zp(d), c), f),
            lambda d: rcopy(
                VS.at[z], FR.at[zp(d)], s_rz.at[d], r_rz.at[zp(d)], dev(x, zp(d), c), f
            ),
        )
        for ds in [(8, 7, 9), (6, 10, 5), (11, 4, 12), (3, 13, 2), (14, 1, 15)]
    ]

    def halo_relay():
        back_g.arrive()
        rows = RW[...].reshape(G * JP * Z, 2 * FD)
        VS[...] = dot_nn(PK[...], rows).astype(BF16).reshape(Z, VR, 2 * FD)
        FR[z] = VS[z]

    h_swap = Exchange(
        range(1, F),
        lambda d: rcopy(HS.at[fp(d)], HR.at[f], s_h.at[d], r_h.at[f], me, fp(d)),
        lambda d: rcopy(HS.at[f], HR.at[fp(d)], s_h.at[d], r_h.at[fp(d)], me, fp(d)),
    )

    def halo_finish():
        for part in back_z:
            part.arrive()
        rows = FR[...].reshape(Z * VR, 2 * FD)
        even = dot_nn(GM[0], rows)
        odd = dot_nn(GM[1], rows)
        halo = even[:, 0:FD] + odd[:, FD : 2 * FD]
        for i in range(F):
            for cl in range(CL):
                at_row = cl * CS + i * RD
                HS[i, cl * RD : (cl + 1) * RD] = halo[at_row : at_row + RD]
        h_swap.begin()
        HR[f] = HS[f]

    op = Exchange([0], lambda _: rcopy(OPS, OPR, s_op.at[0], r_op.at[0], dev(xp(2), z, c), f))
    parts = [(par, b) for b in range(ND // KB) for par in range(2)]

    def far_sum():
        OPS[...] = chain_end(0).astype(BF16)
        op.begin()

    work = {
        "P": products,
        "X": send_x,
        "A": lambda r: chain_step(0, r),
        "B": lambda r: chain_step(1, r),
        "W": lambda _: halo_wants(),
        "H": lambda i: halo_part(*parts[i]),
        "G": lambda _: halo_answer(),
        "R": lambda _: halo_relay(),
        "S": lambda i: back_z[i].begin(),
        "F": lambda _: halo_finish(),
        "E": lambda _: far_sum(),
    }
    for item in ORDER:
        work[item[0]](int(item[1]))

    w_swap.arrive()
    h_swap.arrive()

    def split(v):
        top = v.astype(BF16)
        return top, (v - top.astype(F32)).astype(BF16)

    act = jnp.zeros((RR, FT), F32)
    for i in range(F):
        top, rest = split(HR[i])
        act += dot_nn(top, WF[i]) + dot_nn(rest, WF[i])
    for side in range(2):
        px[0, 0, side].arrive()
    total = chain_end(1)
    op.arrive()
    top, rest = split(total + OPR[...].astype(F32))
    weight = WF[...].reshape(FT, FT)
    act += dot_nn(top, weight) + dot_nn(rest, weight)
    out = act / (1.0 + jnp.exp(-act))

    o_swap = Exchange(
        range(1, F),
        lambda d: rcopy(OS.at[fp(d)], o_ref.at[f], s_o.at[d], r_o.at[f], me, fp(d)),
        lambda d: rcopy(OS.at[f], o_ref.at[fp(d)], s_o.at[d], r_o.at[fp(d)], me, fp(d)),
    )
    for i in range(F):
        OS[i] = out[:, i * FD : (i + 1) * FD].astype(BF16)
    o_swap.begin()
    o_ref[f] = OS[f]
    finish_all()


def per_device(F, x_batch, tiles, tile_src, tile_dst, history, halo_ids, halo_adj, weight):
    N = tile_dst.shape[0]
    Z = N // G
    FD = x_batch.shape[1]
    FT = F * FD
    ND = history.shape[0]
    RD = CS // F
    RR = CL * RD
    H = Z // 2
    src_t = tile_src.reshape(N, K).T
    dst_t = tile_dst.reshape(N, K).T
    tiles_v = tiles.reshape(X, Z, C, K, RD, CS)
    vmem = pl.BlockSpec(memory_space=pltpu.VMEM)
    hbm = pl.BlockSpec(memory_space=pltpu.HBM)
    dma = pltpu.SemaphoreType.DMA
    mmax = 2 * X * K * RD
    out = pl.pallas_call(
        functools.partial(layer_kernel, Z, F, FD, ND, CUT),
        out_shape=jax.ShapeDtypeStruct((F, RR, FD), BF16),
        in_specs=[hbm] * 8,
        out_specs=vmem,
        scratch_shapes=[
            pltpu.VMEM((FD, CL * CS), BF16),
            pltpu.VMEM((K, N), I32),
            pltpu.VMEM((K, N), I32),
            pltpu.VMEM((FD, ND), BF16),
            pltpu.VMEM((CL, CS), I32),
            pltpu.VMEM((CL, CS, CS), BF16),
            pltpu.VMEM((FD, FT), BF16),
            pltpu.VMEM((C, X, Z, K, RD, CS), BF16),
            pltpu.VMEM((C, K, N), I32),
            pltpu.SMEM((C, K, N), I32),
            pltpu.VMEM((C, FT, CL * CS), BF16),
            pltpu.VMEM((C, CL * CS, FT), BF16),
            pltpu.VMEM((F, FD, FT), BF16),
            pltpu.VMEM((Z, 1, G * PAIR), I32),
            pltpu.VMEM((Z, 1, G * PAIR), I32),
            pltpu.VMEM((Z, G * PAIR), I32),
            pltpu.VMEM((C, X, Z, G * PAIR), I32),
            pltpu.SMEM((X, Z, G * PAIR), I32),
            pltpu.VMEM((2, ND, 2 * FD), BF16),
            pltpu.VMEM((SLOTS, G * Z, CS), I32),
            pltpu.VMEM((JP * G * Z, 2 * FD), F32),
            pltpu.VMEM((Z * VR, G * JP * Z), BF16),
            pltpu.VMEM((C, X, JP, Z, 2 * FD), BF16),
            pltpu.VMEM((C, X, JP, Z, 2 * FD), BF16),
            pltpu.VMEM((Z, VR, 2 * FD), BF16),
            pltpu.VMEM((Z, VR, 2 * FD), BF16),
            pltpu.VMEM((2, CL * CS, Z * VR), BF16),
            pltpu.VMEM((F, RR, FD), F32),
            pltpu.VMEM((F, RR, FD), F32),
            pltpu.VMEM((C, mmax, CL * CS), BF16),
            pltpu.VMEM((C, mmax, FT), F32),
            pltpu.VMEM((H + 1, 2, X, RR, FT), F32),
            pltpu.VMEM((H + 1, 2, 2, RR, FT), BF16),
            pltpu.VMEM((H + 1, 2, 2, RR, FT), BF16),
            pltpu.VMEM((2, 2, H, RR, FT), BF16),
            pltpu.VMEM((2, 2, H, RR, FT), BF16),
            pltpu.VMEM((RR, FT), BF16),
            pltpu.VMEM((RR, FT), BF16),
            pltpu.VMEM((F, RR, FD), BF16),
            dma((10,)),
            dma((Z,)), dma((Z,)),
            dma((G,)), dma((C, X)),
            dma((F, C)), dma((C, F)),
            dma((F,)), dma((F,)),
            dma((1,)), dma((1,)),
            dma((1,)), dma((1,)),
            dma((H + 1, 2, 2)), dma((H + 1, 2, 2)),
            dma((2, 2, H)), dma((2, 2, H)),
            dma((1,)), dma((1,)),
            dma((G,)), dma((C, X)),
            dma((Z,)), dma((Z,)),
            dma((F,)), dma((F,)),
            dma((F,)), dma((F,)),
        ],
        compiler_params=pltpu.CompilerParams(
            collective_id=0, has_side_effects=True, vmem_limit_bytes=60 * 1024 * 1024
        ),
        name="layer",
    )(x_batch.T, tiles_v, src_t, dst_t, history.T, halo_ids, halo_adj, weight)
    return out.reshape(F, CL, RD, FD).transpose(1, 0, 2, 3).reshape(CL * CS, FD)


def solution(mesh):
    return jax.shard_map(
        functools.partial(per_device, mesh.shape["feat"]),
        mesh=mesh,
        in_specs=(
            P("nodes", "feat"),
            P("nodes", None, None, "feat", None),
            P("nodes", None, None),
            P(None, "nodes", None),
            P("nodes", "feat"),
            P("nodes", None),
            P("nodes", None, None),
            P("feat", None),
        ),
        out_specs=P("nodes", "feat"),
        check_vma=False,
    )
```

```python
import functools

import jax
import jax.numpy as jnp
from jax import lax
from jax.experimental import pallas as pl
from jax.experimental.pallas import tpu as pltpu
from jax.sharding import PartitionSpec as P

MESH = pl.DeviceIdType.MESH
F32 = jnp.float32
BF16 = jnp.bfloat16
I32 = jnp.int32

X = 4
C = 2
G = X * C
CL = 3
K = 2
CS = 128
STEP = (1, 2, 1, 2, 1, 2, 1, 2)
ORDER = [
    "P8", "X8", "P7", "X7", "P6", "X6", "W0", "H0", "H1", "H2", "H3", "H4", "H5", "H6", "H7",
    "G0", "Y8", "Y7", "P5", "X5", "Y6", "P4", "X4", "B8", "B7", "R0", "S0", "Y5", "P3", "X3",
    "B6", "S1", "Y4", "P2", "X2", "S2", "B5", "Y3", "P1", "X1", "B4", "S3", "Y2", "P0", "X0",
    "B3", "S4", "Y1", "Y0", "B2", "F0", "B1",
]
SLOTS = 9
PAIR = 16
JP = 5
VR = 48
MARK = 4096


def iota(shape, dim):
    return lax.broadcasted_iota(I32, shape, dim)


def dot_nt(a, b):
    return lax.dot_general(a, b, (((1,), (1,)), ((), ())), preferred_element_type=F32)


def dot_nn(a, b):
    return jnp.dot(a, b, preferred_element_type=F32)


def layer_kernel(
    Z, F, FD, ND,
    x_hbm, tiles_ref, src_hbm, dst_hbm, hist_hbm, ids_hbm, adj_hbm, w_hbm, o_ref,
    XI, SI, DI, HI, II, AI, WI,
    TV, SV, SSM, XT, XM, WF, ST, ZR, ZR2, AG, ASM, H2, WB, HACC, PK, RS, RW, VS, FR, GM, HS, HR,
    LH, OB, PO, OXS, OXR, PXS, PXR, CHS, CHR, OS,
    loc, s_z, r_z, s_g, r_g, s_x, r_x, s_w, r_w, s_t, r_t, s_v, r_v, s_ox, r_ox, s_px, r_px, s_c, r_c,
    s_rg, r_rg, s_rz, r_rz, s_h, r_h, s_o, r_o,
):
    N = X * Z * C
    FT = F * FD
    RD = CS // F
    RR = CL * RD
    H = Z // 2
    ZB = Z.bit_length() - 1
    NB = ND.bit_length() - 1

    me = lax.axis_index("nodes")
    f = lax.axis_index("feat")
    c = lax.rem(me, C)
    z = lax.rem(me // C, Z)
    x = me // (C * Z)
    oc = 1 - c
    sib = (x * Z + z) * C + oc

    def dev(xx, zz, cc):
        return (xx * Z + zz) * C + cc

    def zp(d):
        return lax.rem(z + d + Z, Z)

    def xp(d):
        return lax.rem(x + d, X)

    def fp(d):
        return lax.rem(f + d, F)

    def rcopy(src, dst, ss, rs, n, ff):
        return pltpu.make_async_remote_copy(
            src_ref=src, dst_ref=dst, send_sem=ss, recv_sem=rs,
            device_id=(n, ff), device_id_type=MESH,
        )

    begun = {}

    class Exchange:
        def __init__(self, steps, send, recv=None, rolled=False):
            self.steps, self.send, self.recv = steps, send, recv or send
            self.rolled = rolled
            self.received = False

        def each(self, act):
            if self.rolled:
                pl.loop(self.steps[0], self.steps[-1] + 1)(act)
            else:
                for step in self.steps:
                    act(step)

        def begin(self):
            begun[id(self)] = self
            self.each(lambda step: self.send(step).start())

        def arrive(self):
            self.received = True
            self.each(lambda step: self.recv(step).wait_recv())

        def finish(self):
            self.each(lambda step: self.send(step).wait_send())

    def finish_all():
        for e in begun.values():
            if not e.received:
                e.arrive()
            e.finish()

    loads = [
        pltpu.make_async_copy(src, dst, loc.at[i])
        for i, (src, dst) in enumerate(
            [
                (ids_hbm, II), (dst_hbm, DI), (src_hbm, SI), (x_hbm, XI), (w_hbm, WI),
                (hist_hbm, HI), (adj_hbm, AI), (tiles_ref.at[:, :, c], TV.at[c]),
            ]
        )
    ]
    for load in loads:
        load.start()
    l_ids, l_dst, l_src, l_x, l_w, l_hist, l_adj, own_tiles = loads

    barrier = pltpu.get_barrier_semaphore()

    def greet(n, ff):
        pl.semaphore_signal(barrier, inc=1, device_id=(n, ff), device_id_type=MESH)

    @pl.loop(1, Z)
    def _(d):
        greet(dev(x, zp(d), c), f)

    for g in range(1, G):
        greet(dev(xp(g // C), z, lax.rem(c + g, C)), f)
    for d in range(1, F):
        greet(me, fp(d))
        greet(sib, fp(d))

    l_ids.wait()
    l_dst.wait()
    ids = II[...]
    nid = CL * CS
    row = jnp.concatenate([ids[i : i + 1] for i in range(CL)], axis=1)
    owner = row >> NB
    local = row & (ND - 1)
    o_c = owner & (C - 1)
    o_z = (owner >> 1) & (Z - 1)
    o_x = owner >> (1 + ZB)
    hot = (iota((N, nid), 0) == owner).astype(F32)
    tri = (iota((nid, nid), 0) < iota((nid, nid), 1)).astype(F32).astype(BF16)
    before = dot_nn(hot.astype(BF16), tri)
    rank = jnp.sum(before * hot, axis=0, keepdims=True).astype(I32)
    lane = (o_x * C + o_c) * PAIR + rank
    lane_hot = (iota((G * PAIR, nid), 0) == lane).astype(F32).astype(BF16)
    z_hot = (iota((Z, nid), 0) == o_z).astype(F32)
    hi = (local >> 7).astype(F32)
    lo = (local & 127).astype(F32)
    table = 128.0 * dot_nt((z_hot * hi).astype(BF16), lane_hot) + dot_nt(
        (z_hot * lo).astype(BF16), lane_hot
    )
    asked = dot_nt(z_hot.astype(BF16), lane_hot)
    holder = iota((1, N), 1)
    h_z = (holder >> 1) & (Z - 1)
    h_l = ((holder >> (1 + ZB)) * C + (holder & 1)) * PAIR + SLOTS
    z_hold = (iota((Z, N), 0) == h_z).astype(F32)
    for k in range(K):
        l_hold = (iota((G * PAIR, N), 0) == h_l + k).astype(F32).astype(BF16)
        code = DI[k : k + 1, :].astype(F32)
        table += dot_nt((z_hold * code).astype(BF16), l_hold)
    table = table.astype(I32) + jnp.where(asked > 0.5, 0, MARK)
    for i in range(Z):
        ST[i] = table[i : i + 1]

    pl.semaphore_wait(barrier, Z - 1 + G - 1 + 2 * (F - 1))

    hop_z = Exchange(
        range(1, Z),
        lambda d: rcopy(ST.at[zp(d)], ZR.at[z], s_z.at[d], r_z.at[z], dev(x, zp(d), c), f),
        lambda d: rcopy(ST.at[z], ZR.at[zp(d)], s_z.at[d], r_z.at[zp(d)], dev(x, zp(d), c), f),
        rolled=True,
    )
    hop_z.begin()

    t_swap = Exchange(
        [0],
        lambda _: rcopy(tiles_ref.at[:, :, oc], TV.at[c], s_t.at[0], r_t.at[0], sib, f),
        lambda _: rcopy(tiles_ref.at[:, :, oc], TV.at[oc], s_t.at[0], r_t.at[0], sib, f),
    )
    v_swap = Exchange(
        [0],
        lambda _: rcopy(src_hbm, SV.at[c], s_v.at[0], r_v.at[0], sib, f),
        lambda _: rcopy(src_hbm, SV.at[oc], s_v.at[0], r_v.at[0], sib, f),
    )

    def x_rows(cc, ff):
        return XT.at[cc, pl.ds(pl.multiple_of(ff * FD, FD), FD)]

    def x_core(e):
        return lax.rem(c + e, C)

    x_swap = Exchange(
        [(d, e) for e in range(C) for d in range(F) if (d, e) != (0, 0)],
        lambda p: rcopy(
            x_hbm, x_rows(c, f), s_x.at[p], r_x.at[c, f], dev(x, z, x_core(p[1])), fp(p[0])
        ),
        lambda p: rcopy(
            x_hbm, x_rows(x_core(p[1]), fp(p[0])), s_x.at[p], r_x.at[x_core(p[1]), fp(p[0])],
            dev(x, z, x_core(p[1])), fp(p[0]),
        ),
    )
    w_swap = Exchange(
        range(1, F),
        lambda d: rcopy(w_hbm, WF.at[f], s_w.at[d], r_w.at[f], me, fp(d)),
        lambda d: rcopy(w_hbm, WF.at[fp(d)], s_w.at[d], r_w.at[fp(d)], me, fp(d)),
    )
    v_swap.begin()
    x_swap.begin()
    t_swap.begin()
    w_swap.begin()
    l_src.wait()
    l_x.wait()
    l_w.wait()
    XT[c, pl.ds(pl.multiple_of(f * FD, FD), FD)] = XI[...]
    WF[f] = WI[...]
    SV[c] = SI[...]
    ZR[z] = ST[z]

    l_hist.wait()
    hist = HI[...]
    zero = jnp.zeros((FD, ND), BF16)
    H2[0] = jnp.concatenate([hist, zero], axis=0).T
    H2[1] = jnp.concatenate([zero, hist], axis=0).T
    l_adj.wait()
    spot = o_z * VR + (o_c * X + o_x) * JP + (rank >> 1)
    for cl in range(CL):
        cols = slice(cl * CS, (cl + 1) * CS)
        hit = iota((Z * VR, CS), 0) == spot[:, cols]
        odd = rank[:, cols] & 1
        for par in range(2):
            pick = jnp.where(hit, (odd == par).astype(F32), 0.0).astype(BF16)
            GM[par, cols] = dot_nt(AI[cl], pick).astype(BF16)

    def relay_rows(i, carry):
        shape = (VR, G * JP * Z)
        pick = (iota(shape, 1) == iota(shape, 0) * Z + i).astype(F32).astype(BF16)
        PK[pl.ds(pl.multiple_of(i * VR, VR), VR)] = pick
        return carry

    lax.fori_loop(0, Z, relay_rows, 0)

    hop_z.arrive()
    for i in range(Z):
        ZR2[i : i + 1, :] = ZR[i]

    def g_peer(g):
        return xp(g // C), lax.rem(c + g, C)

    def g_send(g):
        gx, gc = g_peer(g)
        return rcopy(ZR2, AG.at[c, x], s_g.at[g], r_g.at[c, x], dev(gx, z, gc), f)

    def g_recv(g):
        gx, gc = g_peer(g)
        return rcopy(ZR2, AG.at[gc, gx], s_g.at[g], r_g.at[gc, gx], dev(gx, z, gc), f)

    hop_g = Exchange(range(1, G), g_send, g_recv)
    hop_g.begin()
    AG[c, x] = ZR2[...]

    x_swap.arrive()
    v_swap.arrive()
    src_copy = pltpu.make_async_copy(SV, SSM, loc.at[8])
    src_copy.start()
    for h in range(C):
        for s in range(CL):
            XM[h, s * CS : (s + 1) * CS, :] = XT[h, :, s * CS : (s + 1) * CS].T
    hop_g.arrive()
    code_copy = pltpu.make_async_copy(AG.at[c], ASM, loc.at[9])
    code_copy.start()
    t_swap.arrive()
    own_tiles.wait()
    src_copy.wait()
    code_copy.wait()

    def dirs_of(r):
        return (0,) if r in (0, H) else (0, 1)

    KR = K * RD

    def products(r):
        count = len(dirs_of(r)) * X

        def place(b):
            bx = lax.rem(b, X)
            step = jnp.where(b < X, r, Z - r)
            return lax.rem(x + bx, X), lax.rem(z + step, Z)

        def gather(b, carry):
            tx, tz = place(b)
            n = dev(tx, tz, c)
            for h in range(C):
                for k in range(K):
                    tile = TV[h, tx, tz, k]
                    src = SSM[h, k, n]
                    rows = pl.ds(pl.multiple_of(b * KR + k * RD, RD), RD)
                    for s in range(CL):
                        LH[h, rows, s * CS : (s + 1) * CS] = jnp.where(
                            src == s, tile, jnp.zeros_like(tile)
                        )
            return carry

        lax.fori_loop(0, count, gather, 0)
        m = count * KR
        for h in range(C):
            OB[h, 0:m] = dot_nn(LH[h, 0:m], XM[h])

        def combine(b, carry):
            tx, tz = place(b)
            bx = lax.rem(b, X)
            bd = b // X
            for d in range(CL):
                total = jnp.zeros((RD, FT), F32)
                for h in range(C):
                    for k in range(K):
                        part = OB[h, pl.ds(pl.multiple_of(b * KR + k * RD, RD), RD)]
                        code = ASM[tx, tz, x * (C * PAIR) + h * PAIR + SLOTS + k] - MARK
                        total += jnp.where(code == d, part, jnp.zeros_like(part))
                PO[r, bd, bx, d * RD : (d + 1) * RD] = total
            return carry

        lax.fori_loop(0, count, combine, 0)

    HF = RR // 2
    halves = (slice(0, HF), slice(HF, RR))
    sides = (1, X - 1)

    def half_of(h):
        return pl.ds(h * HF, HF)

    def ox_copy(p):
        to = xp(sides[p[2]])
        return rcopy(OXS.at[p], OXR.at[p], s_ox.at[p], r_ox.at[p], dev(to, z, c), f)

    def px_copy(p):
        to = xp(sides[p[2]])
        at_p = (p[0], p[1], p[2], half_of(p[3]))
        return rcopy(PXS.at[at_p], PXR.at[at_p], s_px.at[p], r_px.at[p], dev(to, z, c), f)

    ways = [(r, d, side) for r in range(H + 1) for d in dirs_of(r) for side in range(2)]
    ox = {p: Exchange([p], ox_copy) for p in ways}
    px = {(*p, h): Exchange([(*p, h)], px_copy) for p in ways for h in range(2)}

    def send_x(r):
        for d in dirs_of(r):
            for side, bx in enumerate(sides):
                OXS[r, d, side] = PO[r, d, 2, halves[side]].astype(BF16)
                ox[r, d, side].begin()
            for side, bx in enumerate(sides):
                rows = halves[1 - side]
                PXS[r, d, side, rows] = PO[r, d, bx, rows].astype(BF16)
                px[r, d, side, 1 - side].begin()

    def send_y(r):
        for d in dirs_of(r):
            for side, bx in enumerate(sides):
                ox[r, d, side].arrive()
                rows = halves[side]
                total = PO[r, d, bx, rows] + OXR[r, d, side].astype(F32)
                PXS[r, d, side, rows] = total.astype(BF16)
                px[r, d, side, side].begin()

    def live(d, r):
        return r < H or (r == H and d == 0)

    def inputs(d, r):
        return [q for q in range(H, r, -1) if live(d, q) and q - STEP[q - 1] == r]

    def chain_copy(p):
        d, at_r = p
        to = zp(STEP[at_r] if d == 0 else -STEP[at_r])
        return rcopy(CHS.at[p], CHR.at[p], s_c.at[p], r_c.at[p], dev(x, to, c), f)

    chain = {
        (d, r): Exchange([(d, r - 1)], chain_copy)
        for d in range(2) for r in range(1, H + 1) if live(d, r)
    }

    def own(r, d):
        for side in range(2):
            for h in range(2):
                px[r, d, side, h].arrive()
        return PO[r, d, 0] + PXR[r, d, 0].astype(F32) + PXR[r, d, 1].astype(F32)

    def chain_step(r):
        for d in dirs_of(r):
            total = own(r, d)
            for q in inputs(d, r):
                chain[d, q].arrive()
                total = total + CHR[d, q - 1].astype(F32)
            CHS[d, r - 1] = total.astype(BF16)
            chain[d, r].begin()

    def chain_end():
        total = own(0, 0)
        for d in range(2):
            for q in inputs(d, 0):
                chain[d, q].arrive()
                total = total + CHR[d, q - 1].astype(F32)
        return total

    def rg_send(g):
        gx, gc = g_peer(g)
        return rcopy(RS.at[gc, gx], RW.at[c, x], s_rg.at[g], r_rg.at[c, x], dev(gx, z, gc), f)

    def rg_recv(g):
        gx, gc = g_peer(g)
        return rcopy(RS.at[c, x], RW.at[gc, gx], s_rg.at[g], r_rg.at[gc, gx], dev(gx, z, gc), f)

    back_g = Exchange(range(1, G), rg_send, rg_recv)

    def halo_wants():
        asks = AG[...].reshape(G * Z, G * PAIR).astype(F32)
        lanes = iota((G * Z, G * PAIR), 1)
        base = x * (C * PAIR) + c * PAIR
        for s in range(SLOTS):
            want = jnp.sum(jnp.where(lanes == base + s, asks, 0.0), axis=1, keepdims=True)
            WB[s] = jnp.broadcast_to(want, (G * Z, CS)).astype(I32)

    KB = min(512, ND)

    def halo_part(par, b):
        slots = range(par, SLOTS, 2)
        wide = iota((G * Z, KB), 1) + b * KB
        pick = jnp.concatenate(
            [
                (wide == jnp.concatenate([WB[s]] * (KB // CS), axis=1)).astype(F32).astype(BF16)
                for s in slots
            ],
            axis=0,
        )
        rows = len(slots) * G * Z
        got = dot_nn(pick, H2[par, b * KB : (b + 1) * KB])
        HACC[0:rows] = got if b == 0 and par == 0 else HACC[0:rows] + got

    def halo_answer():
        for j in range(JP):
            got = HACC[j * G * Z : (j + 1) * G * Z].astype(BF16)
            RS[:, :, j] = got.reshape(C, X, Z, 2 * FD)
        back_g.begin()
        RW[c, x] = RS[c, x]

    back_z = [
        Exchange(
            ds,
            lambda d: rcopy(VS.at[zp(d)], FR.at[z], s_rz.at[d], r_rz.at[z], dev(x, zp(d), c), f),
            lambda d: rcopy(
                VS.at[z], FR.at[zp(d)], s_rz.at[d], r_rz.at[zp(d)], dev(x, zp(d), c), f
            ),
        )
        for ds in [(8, 7, 9), (6, 10, 5), (11, 4, 12), (3, 13, 2), (14, 1, 15)]
    ]

    def halo_relay():
        back_g.arrive()
        rows = RW[...].reshape(G * JP * Z, 2 * FD)
        VS[...] = dot_nn(PK[...], rows).astype(BF16).reshape(Z, VR, 2 * FD)
        FR[z] = VS[z]

    h_swap = Exchange(
        range(1, F),
        lambda d: rcopy(HS.at[fp(d)], HR.at[f], s_h.at[d], r_h.at[f], me, fp(d)),
        lambda d: rcopy(HS.at[f], HR.at[fp(d)], s_h.at[d], r_h.at[fp(d)], me, fp(d)),
    )

    def halo_finish():
        for part in back_z:
            part.arrive()
        rows = FR[...].reshape(Z * VR, 2 * FD)
        even = dot_nn(GM[0], rows)
        odd = dot_nn(GM[1], rows)
        halo = even[:, 0:FD] + odd[:, FD : 2 * FD]
        for i in range(F):
            for cl in range(CL):
                at_row = cl * CS + i * RD
                HS[i, cl * RD : (cl + 1) * RD] = halo[at_row : at_row + RD]
        h_swap.begin()
        HR[f] = HS[f]

    parts = [(par, b) for b in range(ND // KB) for par in range(2)]

    work = {
        "P": products,
        "X": send_x,
        "Y": send_y,
        "B": chain_step,
        "W": lambda _: halo_wants(),
        "H": lambda i: halo_part(*parts[i]),
        "G": lambda _: halo_answer(),
        "R": lambda _: halo_relay(),
        "S": lambda i: back_z[i].begin(),
        "F": lambda _: halo_finish(),
    }
    for item in ORDER:
        work[item[0]](int(item[1]))

    w_swap.arrive()
    h_swap.arrive()

    def split(v):
        top = v.astype(BF16)
        return top, (v - top.astype(F32)).astype(BF16)

    act = jnp.zeros((RR, FT), F32)
    for i in range(F):
        top, rest = split(HR[i])
        act += dot_nn(top, WF[i]) + dot_nn(rest, WF[i])
    top, rest = split(chain_end())
    weight = WF[...].reshape(FT, FT)
    act += dot_nn(top, weight) + dot_nn(rest, weight)
    out = act / (1.0 + jnp.exp(-act))

    o_swap = Exchange(
        range(1, F),
        lambda d: rcopy(OS.at[fp(d)], o_ref.at[f], s_o.at[d], r_o.at[f], me, fp(d)),
        lambda d: rcopy(OS.at[f], o_ref.at[fp(d)], s_o.at[d], r_o.at[fp(d)], me, fp(d)),
    )
    for i in range(F):
        OS[i] = out[:, i * FD : (i + 1) * FD].astype(BF16)
    o_swap.begin()
    o_ref[f] = OS[f]
    finish_all()


def per_device(F, x_batch, tiles, tile_src, tile_dst, history, halo_ids, halo_adj, weight):
    N = tile_dst.shape[0]
    Z = N // G
    FD = x_batch.shape[1]
    FT = F * FD
    ND = history.shape[0]
    RD = CS // F
    RR = CL * RD
    H = Z // 2
    src_t = tile_src.reshape(N, K).T
    dst_t = tile_dst.reshape(N, K).T
    tiles_v = tiles.reshape(X, Z, C, K, RD, CS)
    vmem = pl.BlockSpec(memory_space=pltpu.VMEM)
    hbm = pl.BlockSpec(memory_space=pltpu.HBM)
    dma = pltpu.SemaphoreType.DMA
    mmax = 2 * X * K * RD
    out = pl.pallas_call(
        functools.partial(layer_kernel, Z, F, FD, ND),
        out_shape=jax.ShapeDtypeStruct((F, RR, FD), BF16),
        in_specs=[hbm] * 8,
        out_specs=vmem,
        scratch_shapes=[
            pltpu.VMEM((FD, CL * CS), BF16),
            pltpu.VMEM((K, N), I32),
            pltpu.VMEM((K, N), I32),
            pltpu.VMEM((FD, ND), BF16),
            pltpu.VMEM((CL, CS), I32),
            pltpu.VMEM((CL, CS, CS), BF16),
            pltpu.VMEM((FD, FT), BF16),
            pltpu.VMEM((C, X, Z, K, RD, CS), BF16),
            pltpu.VMEM((C, K, N), I32),
            pltpu.SMEM((C, K, N), I32),
            pltpu.VMEM((C, FT, CL * CS), BF16),
            pltpu.VMEM((C, CL * CS, FT), BF16),
            pltpu.VMEM((F, FD, FT), BF16),
            pltpu.VMEM((Z, 1, G * PAIR), I32),
            pltpu.VMEM((Z, 1, G * PAIR), I32),
            pltpu.VMEM((Z, G * PAIR), I32),
            pltpu.VMEM((C, X, Z, G * PAIR), I32),
            pltpu.SMEM((X, Z, G * PAIR), I32),
            pltpu.VMEM((2, ND, 2 * FD), BF16),
            pltpu.VMEM((SLOTS, G * Z, CS), I32),
            pltpu.VMEM((JP * G * Z, 2 * FD), F32),
            pltpu.VMEM((Z * VR, G * JP * Z), BF16),
            pltpu.VMEM((C, X, JP, Z, 2 * FD), BF16),
            pltpu.VMEM((C, X, JP, Z, 2 * FD), BF16),
            pltpu.VMEM((Z, VR, 2 * FD), BF16),
            pltpu.VMEM((Z, VR, 2 * FD), BF16),
            pltpu.VMEM((2, CL * CS, Z * VR), BF16),
            pltpu.VMEM((F, RR, FD), F32),
            pltpu.VMEM((F, RR, FD), F32),
            pltpu.VMEM((C, mmax, CL * CS), BF16),
            pltpu.VMEM((C, mmax, FT), F32),
            pltpu.VMEM((H + 1, 2, X, RR, FT), F32),
            pltpu.VMEM((H + 1, 2, 2, RR // 2, FT), BF16),
            pltpu.VMEM((H + 1, 2, 2, RR // 2, FT), BF16),
            pltpu.VMEM((H + 1, 2, 2, RR, FT), BF16),
            pltpu.VMEM((H + 1, 2, 2, RR, FT), BF16),
            pltpu.VMEM((2, H, RR, FT), BF16),
            pltpu.VMEM((2, H, RR, FT), BF16),
            pltpu.VMEM((F, RR, FD), BF16),
            dma((10,)),
            dma((Z,)), dma((Z,)),
            dma((G,)), dma((C, X)),
            dma((F, C)), dma((C, F)),
            dma((F,)), dma((F,)),
            dma((1,)), dma((1,)),
            dma((1,)), dma((1,)),
            dma((H + 1, 2, 2)), dma((H + 1, 2, 2)),
            dma((H + 1, 2, 2, 2)), dma((H + 1, 2, 2, 2)),
            dma((2, H)), dma((2, H)),
            dma((G,)), dma((C, X)),
            dma((Z,)), dma((Z,)),
            dma((F,)), dma((F,)),
            dma((F,)), dma((F,)),
        ],
        compiler_params=pltpu.CompilerParams(
            collective_id=0, has_side_effects=True, vmem_limit_bytes=60 * 1024 * 1024
        ),
        name="layer",
    )(x_batch.T, tiles_v, src_t, dst_t, history.T, halo_ids, halo_adj, weight)
    return out.reshape(F, CL, RD, FD).transpose(1, 0, 2, 3).reshape(CL * CS, FD)


def solution(mesh):
    return jax.shard_map(
        functools.partial(per_device, mesh.shape["feat"]),
        mesh=mesh,
        in_specs=(
            P("nodes", "feat"),
            P("nodes", None, None, "feat", None),
            P("nodes", None, None),
            P(None, "nodes", None),
            P("nodes", "feat"),
            P("nodes", None),
            P("nodes", None, None),
            P("feat", None),
        ),
        out_specs=P("nodes", "feat"),
        check_vma=False,
    )
```

```python
import functools

import jax
import jax.numpy as jnp
from jax import lax
from jax.experimental import pallas as pl
from jax.experimental.pallas import tpu as pltpu
from jax.sharding import PartitionSpec as P

MESH = pl.DeviceIdType.MESH
F32 = jnp.float32
BF16 = jnp.bfloat16
I32 = jnp.int32

X = 4
C = 2
G = X * C
CL = 3
K = 2
CS = 128
STEP = (1, 2, 1, 2, 1, 2, 1, 2)
ORDER = [
    "P8", "X8", "P7", "X7", "P6", "X6", "W0", "H0", "H1", "H2", "H3", "H4", "H5", "H6", "H7",
    "G0", "Y8", "Y7", "P5", "X5", "Y6", "P4", "X4", "B8", "B7", "R0", "S0", "Y5", "P3", "X3",
    "B6", "S1", "Y4", "P2", "X2", "S2", "B5", "Y3", "P1", "X1", "B4", "S3", "Y2", "P0", "X0",
    "B3", "S4", "Y1", "Y0", "B2", "F0", "B1",
]
SLOTS = 9
PAIR = 16
JP = 5
VR = 48
MARK = 4096


def iota(shape, dim):
    return lax.broadcasted_iota(I32, shape, dim)


def dot_nt(a, b):
    return lax.dot_general(a, b, (((1,), (1,)), ((), ())), preferred_element_type=F32)


def dot_nn(a, b):
    return jnp.dot(a, b, preferred_element_type=F32)


def layer_kernel(
    Z, F, FD, ND,
    x_hbm, tiles_ref, src_hbm, dst_hbm, hist_hbm, ids_hbm, adj_hbm, w_hbm, o_ref,
    XI, SI, DI, HI, II, AI, WI,
    TV, SV, SSM, XT, XM, WF, ST, ZR, ZR2, AG, ASM, H2, WB, HACC, PK, RS, RW, VS, FR, GM, HS, HR,
    LH, OB, PO, OXS, OXR, PXS, PXR, CHS, CHR, OS,
    loc, s_z, r_z, s_g, r_g, s_x, r_x, s_w, r_w, s_t, r_t, s_v, r_v, s_ox, r_ox, s_px, r_px, s_c, r_c,
    s_rg, r_rg, s_rz, r_rz, s_h, r_h, s_o, r_o,
):
    N = X * Z * C
    FT = F * FD
    RD = CS // F
    RR = CL * RD
    H = Z // 2
    ZB = Z.bit_length() - 1
    NB = ND.bit_length() - 1

    me = lax.axis_index("nodes")
    f = lax.axis_index("feat")
    c = lax.rem(me, C)
    z = lax.rem(me // C, Z)
    x = me // (C * Z)
    oc = 1 - c
    sib = (x * Z + z) * C + oc
    FAR = sorted(range(1, Z), key=lambda d: -min(d, Z - d))

    def dev(xx, zz, cc):
        return (xx * Z + zz) * C + cc

    def zp(d):
        return lax.rem(z + d + Z, Z)

    def xp(d):
        return lax.rem(x + d, X)

    def fp(d):
        return lax.rem(f + d, F)

    def rcopy(src, dst, ss, rs, n, ff):
        return pltpu.make_async_remote_copy(
            src_ref=src, dst_ref=dst, send_sem=ss, recv_sem=rs,
            device_id=(n, ff), device_id_type=MESH,
        )

    begun = {}

    class Exchange:
        def __init__(self, steps, send, recv=None, rolled=False):
            self.steps, self.send, self.recv = steps, send, recv or send
            self.rolled = rolled
            self.received = False

        def each(self, act):
            if self.rolled:
                pl.loop(self.steps[0], self.steps[-1] + 1)(act)
            else:
                for step in self.steps:
                    act(step)

        def begin(self):
            begun[id(self)] = self
            self.each(lambda step: self.send(step).start())

        def arrive(self):
            self.received = True
            self.each(lambda step: self.recv(step).wait_recv())

        def finish(self):
            self.each(lambda step: self.send(step).wait_send())

    def finish_all():
        for e in begun.values():
            if not e.received:
                e.arrive()
            e.finish()

    loads = [
        pltpu.make_async_copy(src, dst, loc.at[i])
        for i, (src, dst) in enumerate(
            [
                (ids_hbm, II), (dst_hbm, DI), (src_hbm, SI), (x_hbm, XI), (w_hbm, WI),
                (hist_hbm, HI), (adj_hbm, AI), (tiles_ref.at[:, :, c], TV.at[c]),
            ]
        )
    ]
    for load in loads:
        load.start()
    l_ids, l_dst, l_src, l_x, l_w, l_hist, l_adj, own_tiles = loads

    barrier = pltpu.get_barrier_semaphore()

    def greet(n, ff):
        pl.semaphore_signal(barrier, inc=1, device_id=(n, ff), device_id_type=MESH)

    for d in FAR:
        greet(dev(x, zp(d), c), f)

    for g in range(1, G):
        greet(dev(xp(g // C), z, lax.rem(c + g, C)), f)
    for d in range(1, F):
        greet(me, fp(d))
        greet(sib, fp(d))

    l_ids.wait()
    l_dst.wait()
    ids = II[...]
    nid = CL * CS
    row = jnp.concatenate([ids[i : i + 1] for i in range(CL)], axis=1)
    owner = row >> NB
    local = row & (ND - 1)
    o_c = owner & (C - 1)
    o_z = (owner >> 1) & (Z - 1)
    o_x = owner >> (1 + ZB)
    hot = (iota((N, nid), 0) == owner).astype(F32)
    tri = (iota((nid, nid), 0) < iota((nid, nid), 1)).astype(F32).astype(BF16)
    before = dot_nn(hot.astype(BF16), tri)
    rank = jnp.sum(before * hot, axis=0, keepdims=True).astype(I32)
    lane = (o_x * C + o_c) * PAIR + rank
    lane_hot = (iota((G * PAIR, nid), 0) == lane).astype(F32).astype(BF16)
    z_hot = (iota((Z, nid), 0) == o_z).astype(F32)
    hi = (local >> 7).astype(F32)
    lo = (local & 127).astype(F32)
    table = 128.0 * dot_nt((z_hot * hi).astype(BF16), lane_hot) + dot_nt(
        (z_hot * lo).astype(BF16), lane_hot
    )
    asked = dot_nt(z_hot.astype(BF16), lane_hot)
    holder = iota((1, N), 1)
    h_z = (holder >> 1) & (Z - 1)
    h_l = ((holder >> (1 + ZB)) * C + (holder & 1)) * PAIR + SLOTS
    z_hold = (iota((Z, N), 0) == h_z).astype(F32)
    for k in range(K):
        l_hold = (iota((G * PAIR, N), 0) == h_l + k).astype(F32).astype(BF16)
        code = DI[k : k + 1, :].astype(F32)
        table += dot_nt((z_hold * code).astype(BF16), l_hold)
    table = table.astype(I32) + jnp.where(asked > 0.5, 0, MARK)
    for i in range(Z):
        ST[i] = table[i : i + 1]

    pl.semaphore_wait(barrier, Z - 1 + G - 1 + 2 * (F - 1))

    hop_z = Exchange(
        FAR,
        lambda d: rcopy(ST.at[zp(d)], ZR.at[z], s_z.at[d], r_z.at[z], dev(x, zp(d), c), f),
        lambda d: rcopy(ST.at[z], ZR.at[zp(d)], s_z.at[d], r_z.at[zp(d)], dev(x, zp(d), c), f),
    )
    hop_z.begin()

    t_swap = Exchange(
        [0],
        lambda _: rcopy(tiles_ref.at[:, :, oc], TV.at[c], s_t.at[0], r_t.at[0], sib, f),
        lambda _: rcopy(tiles_ref.at[:, :, oc], TV.at[oc], s_t.at[0], r_t.at[0], sib, f),
    )
    v_swap = Exchange(
        [0],
        lambda _: rcopy(src_hbm, SV.at[c], s_v.at[0], r_v.at[0], sib, f),
        lambda _: rcopy(src_hbm, SV.at[oc], s_v.at[0], r_v.at[0], sib, f),
    )

    def x_rows(cc, ff):
        return XT.at[cc, pl.ds(pl.multiple_of(ff * FD, FD), FD)]

    def x_core(e):
        return lax.rem(c + e, C)

    x_swap = Exchange(
        [(d, e) for e in range(C) for d in range(F) if (d, e) != (0, 0)],
        lambda p: rcopy(
            x_hbm, x_rows(c, f), s_x.at[p], r_x.at[c, f], dev(x, z, x_core(p[1])), fp(p[0])
        ),
        lambda p: rcopy(
            x_hbm, x_rows(x_core(p[1]), fp(p[0])), s_x.at[p], r_x.at[x_core(p[1]), fp(p[0])],
            dev(x, z, x_core(p[1])), fp(p[0]),
        ),
    )
    w_swap = Exchange(
        range(1, F),
        lambda d: rcopy(w_hbm, WF.at[f], s_w.at[d], r_w.at[f], me, fp(d)),
        lambda d: rcopy(w_hbm, WF.at[fp(d)], s_w.at[d], r_w.at[fp(d)], me, fp(d)),
    )
    v_swap.begin()
    x_swap.begin()
    t_swap.begin()
    w_swap.begin()
    l_src.wait()
    l_x.wait()
    l_w.wait()
    XT[c, pl.ds(pl.multiple_of(f * FD, FD), FD)] = XI[...]
    WF[f] = WI[...]
    SV[c] = SI[...]
    ZR[z] = ST[z]

    l_hist.wait()
    hist = HI[...]
    zero = jnp.zeros((FD, ND), BF16)
    H2[0] = jnp.concatenate([hist, zero], axis=0).T
    H2[1] = jnp.concatenate([zero, hist], axis=0).T
    l_adj.wait()
    spot = o_z * VR + (o_c * X + o_x) * JP + (rank >> 1)
    for cl in range(CL):
        cols = slice(cl * CS, (cl + 1) * CS)
        hit = iota((Z * VR, CS), 0) == spot[:, cols]
        odd = rank[:, cols] & 1
        for par in range(2):
            pick = jnp.where(hit, (odd == par).astype(F32), 0.0).astype(BF16)
            GM[par, cols] = dot_nt(AI[cl], pick).astype(BF16)

    def relay_rows(i, carry):
        shape = (VR, G * JP * Z)
        pick = (iota(shape, 1) == iota(shape, 0) * Z + i).astype(F32).astype(BF16)
        PK[pl.ds(pl.multiple_of(i * VR, VR), VR)] = pick
        return carry

    lax.fori_loop(0, Z, relay_rows, 0)

    hop_z.arrive()
    for i in range(Z):
        ZR2[i : i + 1, :] = ZR[i]

    def g_peer(g):
        return xp(g // C), lax.rem(c + g, C)

    def g_send(g):
        gx, gc = g_peer(g)
        return rcopy(ZR2, AG.at[c, x], s_g.at[g], r_g.at[c, x], dev(gx, z, gc), f)

    def g_recv(g):
        gx, gc = g_peer(g)
        return rcopy(ZR2, AG.at[gc, gx], s_g.at[g], r_g.at[gc, gx], dev(gx, z, gc), f)

    hop_g = Exchange(range(1, G), g_send, g_recv)
    hop_g.begin()
    AG[c, x] = ZR2[...]

    x_swap.arrive()
    v_swap.arrive()
    src_copy = pltpu.make_async_copy(SV, SSM, loc.at[8])
    src_copy.start()
    for h in range(C):
        for s in range(CL):
            XM[h, s * CS : (s + 1) * CS, :] = XT[h, :, s * CS : (s + 1) * CS].T
    hop_g.arrive()
    code_copy = pltpu.make_async_copy(AG.at[c], ASM, loc.at[9])
    code_copy.start()
    t_swap.arrive()
    own_tiles.wait()
    src_copy.wait()
    code_copy.wait()

    def dirs_of(r):
        return (0,) if r in (0, H) else (0, 1)

    KR = K * RD

    def products(r):
        count = len(dirs_of(r)) * X

        def place(b):
            bx = lax.rem(b, X)
            step = jnp.where(b < X, r, Z - r)
            return lax.rem(x + bx, X), lax.rem(z + step, Z)

        def gather(b, carry):
            tx, tz = place(b)
            n = dev(tx, tz, c)
            for h in range(C):
                for k in range(K):
                    tile = TV[h, tx, tz, k]
                    src = SSM[h, k, n]
                    rows = pl.ds(pl.multiple_of(b * KR + k * RD, RD), RD)
                    for s in range(CL):
                        LH[h, rows, s * CS : (s + 1) * CS] = jnp.where(
                            src == s, tile, jnp.zeros_like(tile)
                        )
            return carry

        lax.fori_loop(0, count, gather, 0)
        m = count * KR
        for h in range(C):
            OB[h, 0:m] = dot_nn(LH[h, 0:m], XM[h])

        def combine(b, carry):
            tx, tz = place(b)
            bx = lax.rem(b, X)
            bd = b // X
            for d in range(CL):
                total = jnp.zeros((RD, FT), F32)
                for h in range(C):
                    for k in range(K):
                        part = OB[h, pl.ds(pl.multiple_of(b * KR + k * RD, RD), RD)]
                        code = ASM[tx, tz, x * (C * PAIR) + h * PAIR + SLOTS + k] - MARK
                        total += jnp.where(code == d, part, jnp.zeros_like(part))
                PO[r, bd, bx, d * RD : (d + 1) * RD] = total
            return carry

        lax.fori_loop(0, count, combine, 0)

    HF = RR // 2
    halves = (slice(0, HF), slice(HF, RR))
    sides = (1, X - 1)

    def half_of(h):
        return pl.ds(h * HF, HF)

    def ox_copy(p):
        to = xp(sides[p[2]])
        return rcopy(OXS.at[p], OXR.at[p], s_ox.at[p], r_ox.at[p], dev(to, z, c), f)

    def px_copy(p):
        to = xp(sides[p[2]])
        at_p = (p[0], p[1], p[2], half_of(p[3]))
        return rcopy(PXS.at[at_p], PXR.at[at_p], s_px.at[p], r_px.at[p], dev(to, z, c), f)

    ways = [(r, d, side) for r in range(H + 1) for d in dirs_of(r) for side in range(2)]
    ox = {p: Exchange([p], ox_copy) for p in ways}
    px = {(*p, h): Exchange([(*p, h)], px_copy) for p in ways for h in range(2)}

    def send_x(r):
        for d in dirs_of(r):
            for side, bx in enumerate(sides):
                OXS[r, d, side] = PO[r, d, 2, halves[side]].astype(BF16)
                ox[r, d, side].begin()
            for side, bx in enumerate(sides):
                rows = halves[1 - side]
                PXS[r, d, side, rows] = PO[r, d, bx, rows].astype(BF16)
                px[r, d, side, 1 - side].begin()

    def send_y(r):
        for d in dirs_of(r):
            for side, bx in enumerate(sides):
                ox[r, d, side].arrive()
                rows = halves[side]
                total = PO[r, d, bx, rows] + OXR[r, d, side].astype(F32)
                PXS[r, d, side, rows] = total.astype(BF16)
                px[r, d, side, side].begin()

    def live(d, r):
        return r < H or (r == H and d == 0)

    def inputs(d, r):
        return [q for q in range(H, r, -1) if live(d, q) and q - STEP[q - 1] == r]

    def chain_copy(p):
        d, at_r = p
        to = zp(STEP[at_r] if d == 0 else -STEP[at_r])
        return rcopy(CHS.at[p], CHR.at[p], s_c.at[p], r_c.at[p], dev(x, to, c), f)

    chain = {
        (d, r): Exchange([(d, r - 1)], chain_copy)
        for d in range(2) for r in range(1, H + 1) if live(d, r)
    }

    def own(r, d):
        for side in range(2):
            for h in range(2):
                px[r, d, side, h].arrive()
        return PO[r, d, 0] + PXR[r, d, 0].astype(F32) + PXR[r, d, 1].astype(F32)

    def chain_step(r):
        for d in dirs_of(r):
            total = own(r, d)
            for q in inputs(d, r):
                chain[d, q].arrive()
                total = total + CHR[d, q - 1].astype(F32)
            CHS[d, r - 1] = total.astype(BF16)
            chain[d, r].begin()

    def chain_end():
        total = own(0, 0)
        for d in range(2):
            for q in inputs(d, 0):
                chain[d, q].arrive()
                total = total + CHR[d, q - 1].astype(F32)
        return total

    def rg_send(g):
        gx, gc = g_peer(g)
        return rcopy(RS.at[gc, gx], RW.at[c, x], s_rg.at[g], r_rg.at[c, x], dev(gx, z, gc), f)

    def rg_recv(g):
        gx, gc = g_peer(g)
        return rcopy(RS.at[c, x], RW.at[gc, gx], s_rg.at[g], r_rg.at[gc, gx], dev(gx, z, gc), f)

    back_g = Exchange(range(1, G), rg_send, rg_recv)

    def halo_wants():
        asks = AG[...].reshape(G * Z, G * PAIR).astype(F32)
        lanes = iota((G * Z, G * PAIR), 1)
        base = x * (C * PAIR) + c * PAIR
        for s in range(SLOTS):
            want = jnp.sum(jnp.where(lanes == base + s, asks, 0.0), axis=1, keepdims=True)
            WB[s] = jnp.broadcast_to(want, (G * Z, CS)).astype(I32)

    KB = min(512, ND)

    def halo_part(par, b):
        slots = range(par, SLOTS, 2)
        wide = iota((G * Z, KB), 1) + b * KB
        pick = jnp.concatenate(
            [
                (wide == jnp.concatenate([WB[s]] * (KB // CS), axis=1)).astype(F32).astype(BF16)
                for s in slots
            ],
            axis=0,
        )
        rows = len(slots) * G * Z
        got = dot_nn(pick, H2[par, b * KB : (b + 1) * KB])
        HACC[0:rows] = got if b == 0 and par == 0 else HACC[0:rows] + got

    def halo_answer():
        for j in range(JP):
            got = HACC[j * G * Z : (j + 1) * G * Z].astype(BF16)
            RS[:, :, j] = got.reshape(C, X, Z, 2 * FD)
        back_g.begin()
        RW[c, x] = RS[c, x]

    back_z = [
        Exchange(
            ds,
            lambda d: rcopy(VS.at[zp(d)], FR.at[z], s_rz.at[d], r_rz.at[z], dev(x, zp(d), c), f),
            lambda d: rcopy(
                VS.at[z], FR.at[zp(d)], s_rz.at[d], r_rz.at[zp(d)], dev(x, zp(d), c), f
            ),
        )
        for ds in [(8, 7, 9), (6, 10, 5), (11, 4, 12), (3, 13, 2), (14, 1, 15)]
    ]

    def halo_relay():
        back_g.arrive()
        rows = RW[...].reshape(G * JP * Z, 2 * FD)
        VS[...] = dot_nn(PK[...], rows).astype(BF16).reshape(Z, VR, 2 * FD)
        FR[z] = VS[z]

    h_swap = Exchange(
        range(1, F),
        lambda d: rcopy(HS.at[fp(d)], HR.at[f], s_h.at[d], r_h.at[f], me, fp(d)),
        lambda d: rcopy(HS.at[f], HR.at[fp(d)], s_h.at[d], r_h.at[fp(d)], me, fp(d)),
    )

    def halo_finish():
        for part in back_z:
            part.arrive()
        rows = FR[...].reshape(Z * VR, 2 * FD)
        even = dot_nn(GM[0], rows)
        odd = dot_nn(GM[1], rows)
        halo = even[:, 0:FD] + odd[:, FD : 2 * FD]
        for i in range(F):
            for cl in range(CL):
                at_row = cl * CS + i * RD
                HS[i, cl * RD : (cl + 1) * RD] = halo[at_row : at_row + RD]
        h_swap.begin()
        HR[f] = HS[f]

    parts = [(par, b) for b in range(ND // KB) for par in range(2)]

    work = {
        "P": products,
        "X": send_x,
        "Y": send_y,
        "B": chain_step,
        "W": lambda _: halo_wants(),
        "H": lambda i: halo_part(*parts[i]),
        "G": lambda _: halo_answer(),
        "R": lambda _: halo_relay(),
        "S": lambda i: back_z[i].begin(),
        "F": lambda _: halo_finish(),
    }
    for item in ORDER:
        work[item[0]](int(item[1]))

    w_swap.arrive()
    h_swap.arrive()

    def split(v):
        top = v.astype(BF16)
        return top, (v - top.astype(F32)).astype(BF16)

    act = jnp.zeros((RR, FT), F32)
    for i in range(F):
        top, rest = split(HR[i])
        act += dot_nn(top, WF[i]) + dot_nn(rest, WF[i])
    top, rest = split(chain_end())
    weight = WF[...].reshape(FT, FT)
    act += dot_nn(top, weight) + dot_nn(rest, weight)
    out = act / (1.0 + jnp.exp(-act))

    o_swap = Exchange(
        range(1, F),
        lambda d: rcopy(OS.at[fp(d)], o_ref.at[f], s_o.at[d], r_o.at[f], me, fp(d)),
        lambda d: rcopy(OS.at[f], o_ref.at[fp(d)], s_o.at[d], r_o.at[fp(d)], me, fp(d)),
    )
    for i in range(F):
        OS[i] = out[:, i * FD : (i + 1) * FD].astype(BF16)
    o_swap.begin()
    o_ref[f] = OS[f]
    finish_all()


def per_device(F, x_batch, tiles, tile_src, tile_dst, history, halo_ids, halo_adj, weight):
    N = tile_dst.shape[0]
    Z = N // G
    FD = x_batch.shape[1]
    FT = F * FD
    ND = history.shape[0]
    RD = CS // F
    RR = CL * RD
    H = Z // 2
    src_t = tile_src.reshape(N, K).T
    dst_t = tile_dst.reshape(N, K).T
    tiles_v = tiles.reshape(X, Z, C, K, RD, CS)
    vmem = pl.BlockSpec(memory_space=pltpu.VMEM)
    hbm = pl.BlockSpec(memory_space=pltpu.HBM)
    dma = pltpu.SemaphoreType.DMA
    mmax = 2 * X * K * RD
    out = pl.pallas_call(
        functools.partial(layer_kernel, Z, F, FD, ND),
        out_shape=jax.ShapeDtypeStruct((F, RR, FD), BF16),
        in_specs=[hbm] * 8,
        out_specs=vmem,
        scratch_shapes=[
            pltpu.VMEM((FD, CL * CS), BF16),
            pltpu.VMEM((K, N), I32),
            pltpu.VMEM((K, N), I32),
            pltpu.VMEM((FD, ND), BF16),
            pltpu.VMEM((CL, CS), I32),
            pltpu.VMEM((CL, CS, CS), BF16),
            pltpu.VMEM((FD, FT), BF16),
            pltpu.VMEM((C, X, Z, K, RD, CS), BF16),
            pltpu.VMEM((C, K, N), I32),
            pltpu.SMEM((C, K, N), I32),
            pltpu.VMEM((C, FT, CL * CS), BF16),
            pltpu.VMEM((C, CL * CS, FT), BF16),
            pltpu.VMEM((F, FD, FT), BF16),
            pltpu.VMEM((Z, 1, G * PAIR), I32),
            pltpu.VMEM((Z, 1, G * PAIR), I32),
            pltpu.VMEM((Z, G * PAIR), I32),
            pltpu.VMEM((C, X, Z, G * PAIR), I32),
            pltpu.SMEM((X, Z, G * PAIR), I32),
            pltpu.VMEM((2, ND, 2 * FD), BF16),
            pltpu.VMEM((SLOTS, G * Z, CS), I32),
            pltpu.VMEM((JP * G * Z, 2 * FD), F32),
            pltpu.VMEM((Z * VR, G * JP * Z), BF16),
            pltpu.VMEM((C, X, JP, Z, 2 * FD), BF16),
            pltpu.VMEM((C, X, JP, Z, 2 * FD), BF16),
            pltpu.VMEM((Z, VR, 2 * FD), BF16),
            pltpu.VMEM((Z, VR, 2 * FD), BF16),
            pltpu.VMEM((2, CL * CS, Z * VR), BF16),
            pltpu.VMEM((F, RR, FD), F32),
            pltpu.VMEM((F, RR, FD), F32),
            pltpu.VMEM((C, mmax, CL * CS), BF16),
            pltpu.VMEM((C, mmax, FT), F32),
            pltpu.VMEM((H + 1, 2, X, RR, FT), F32),
            pltpu.VMEM((H + 1, 2, 2, RR // 2, FT), BF16),
            pltpu.VMEM((H + 1, 2, 2, RR // 2, FT), BF16),
            pltpu.VMEM((H + 1, 2, 2, RR, FT), BF16),
            pltpu.VMEM((H + 1, 2, 2, RR, FT), BF16),
            pltpu.VMEM((2, H, RR, FT), BF16),
            pltpu.VMEM((2, H, RR, FT), BF16),
            pltpu.VMEM((F, RR, FD), BF16),
            dma((10,)),
            dma((Z,)), dma((Z,)),
            dma((G,)), dma((C, X)),
            dma((F, C)), dma((C, F)),
            dma((F,)), dma((F,)),
            dma((1,)), dma((1,)),
            dma((1,)), dma((1,)),
            dma((H + 1, 2, 2)), dma((H + 1, 2, 2)),
            dma((H + 1, 2, 2, 2)), dma((H + 1, 2, 2, 2)),
            dma((2, H)), dma((2, H)),
            dma((G,)), dma((C, X)),
            dma((Z,)), dma((Z,)),
            dma((F,)), dma((F,)),
            dma((F,)), dma((F,)),
        ],
        compiler_params=pltpu.CompilerParams(
            collective_id=0, has_side_effects=True, vmem_limit_bytes=60 * 1024 * 1024
        ),
        name="layer",
    )(x_batch.T, tiles_v, src_t, dst_t, history.T, halo_ids, halo_adj, weight)
    return out.reshape(F, CL, RD, FD).transpose(1, 0, 2, 3).reshape(CL * CS, FD)


def solution(mesh):
    return jax.shard_map(
        functools.partial(per_device, mesh.shape["feat"]),
        mesh=mesh,
        in_specs=(
            P("nodes", "feat"),
            P("nodes", None, None, "feat", None),
            P("nodes", None, None),
            P(None, "nodes", None),
            P("nodes", "feat"),
            P("nodes", None),
            P("nodes", None, None),
            P("feat", None),
        ),
        out_specs=P("nodes", "feat"),
        check_vma=False,
    )
```
